32 devices in a mesh: groups: 2 (over y), xt: 4 (over z), yt: 2 (over x), sg: 2 (over core).
Axes of the slice: x: 2, y: 2, z: 4, core: 2. Of those that a mesh axis runs over, the one named last changes fastest.
Arguments:
- field: float32 [2, 2048, 512], P(None, ('groups', 'xt'), 'yt'), parts along dimension 1, may hold values from -6 to 6
- probe: bfloat16 [8, 2, 256, 256], P('groups'), parts along dimension 0, may hold values from -3 to 3
- amplitudes: bfloat16 [8, 2, 6, 256, 256], P(('groups', 'xt'), 'yt', 'sg'), parts along dimension 0, may hold values from 0.25 to 2.5
- offsets: int32 [8, 2, 6, 2], P(('groups', 'xt'), 'yt', 'sg'), parts along dimension 0, may hold values from 0 to 256, as said below
- counts: int32 [8, 2], P(('groups', 'xt'), 'yt'), parts along dimension 0, may hold values from 1 to 6, as said below
Outputs:
- new_field: float32 [2, 2048, 512], P(None, ('groups', 'xt', 'sg'), 'yt'), parts along dimension 1
- new_probe: float32 [8, 2, 256, 256], P('groups'), parts along dimension 0
The draws below stay inside these ranges and needn't reach their ends.
There are 2 independent parts, one for each index of `groups`. The reference program is written for one: setup_inputs(seed, part) draws one part's arguments, and reference() takes and returns one part's arrays. A program takes and returns all parts, laid end to end along the dimension named above; each array names one. Nothing has to cross between parts.
Inputs may be any that keep to these rules, and one draw needn't show every extreme that they name: `offsets`: each scan window lies within the tile extended by 128 pixels on every side. `counts`: the live scans of a tile are its first slots.
All inputs are finite; a program needn't handle non-finite values.
Results may differ from the reference program's by a relative error of at most 0.0077.
Values sent between devices are 32-bit elements; how exact they have to be, the bound alone decides.
No kernel may reach another device: no remote copies, remote signals or barrier semaphores. Data moves between devices by JAX's collectives and lax.ppermute only.
A program may use at most 64 MiB of HBM per device.

```python
import math
import jax
import jax.numpy as jnp
from jax import lax

P_SIZE = 256
MODES = 4
TILE = 256
SLOTS = 6
OX = 1024
OY = 512
N_XT = 4
N_YT = 2


def draw_offsets(key, part):
    key = jax.random.fold_in(key, 11)
    first_key, second_key, third_key = jax.random.split(key, 3)
    total = N_XT * N_YT * SLOTS * 2
    values_flat = jax.random.randint(first_key, (total,), 0, TILE + 1)
    top_index = jax.random.randint(second_key, (), 0, total)
    step_away = jax.random.randint(third_key, (), 1, total)
    low_index = (top_index + step_away) % total
    values_flat = values_flat.at[top_index].set(TILE)
    values_flat = values_flat.at[low_index].set(0)
    return values_flat.reshape(N_XT, N_YT, SLOTS, 2).astype(jnp.int32)


def draw_counts(key, part):
    key = jax.random.fold_in(key, 23)
    first_key, second_key, third_key = jax.random.split(key, 3)
    total = N_XT * N_YT
    values_flat = jax.random.randint(first_key, (total,), 1, SLOTS + 1)
    top_index = jax.random.randint(second_key, (), 0, total)
    step_away = jax.random.randint(third_key, (), 1, total)
    low_index = (top_index + step_away) % total
    values_flat = values_flat.at[top_index].set(SLOTS)
    values_flat = values_flat.at[low_index].set(1)
    return values_flat.reshape(N_XT, N_YT).astype(jnp.int32)


def level_of(stream_key, shape, pieces, low, top_value):
    factor_of, own = 1.0, jax.random.fold_in(stream_key, 6)
    for axis_at, blocks in pieces:
        heights = jnp.exp(jax.random.uniform(jax.random.fold_in(own, axis_at), (blocks,), jnp.float32, low / len(pieces), top_value / len(pieces)))
        factor_of = factor_of * jnp.repeat(heights, shape[axis_at] // blocks).reshape([-1 if axis == axis_at else 1 for axis in range(len(shape))])
    return factor_of


def gaussian(own_key, extent, spread, reach, pieces=(), kind=jnp.bfloat16):
    array = spread * jax.random.normal(own_key, extent, jnp.float32)
    if pieces:
        array = array * level_of(own_key, extent, pieces, -0.22, 0.18)
    return jnp.clip(array, -reach, reach).astype(kind)


def setup_inputs(seed: int = 0, part: int = 0) -> dict:
    seeds = jax.random.split(jax.random.key(seed), 6)
    own_keys = jax.random.split(jax.random.fold_in(seeds[5], part), 6)
    return {
        "field": gaussian(own_keys[0], (2, OX, OY), 1.0, 6.0, ((1, 4), (2, 2)), jnp.float32),
        "probe": gaussian(own_keys[1], (MODES, 2, P_SIZE, P_SIZE), 0.5, 3.0),
        "amplitudes": jnp.clip(0.25 + 2.25 * jax.random.uniform(own_keys[2], (N_XT, N_YT, SLOTS, P_SIZE, P_SIZE), jnp.float32) ** level_of(own_keys[2], (N_XT, N_YT, SLOTS, P_SIZE, P_SIZE), ((0, 4), (1, 2), (2, 2)), -0.2, 0.2), 0.25, 2.5).astype(jnp.bfloat16),
        "offsets": draw_offsets(jax.random.fold_in(jax.random.fold_in(seeds[5], part), 71), part),
        "counts": draw_counts(jax.random.fold_in(jax.random.fold_in(seeds[5], part), 71), part),
    }


floor_term = 0.5
field_rate = 0.25
probe_rate = 0.1

def dft_tables(width):
    index = jnp.arange(width, dtype=jnp.int32)
    phase = index[:, None] * index[None, :] % width
    angle = phase.astype(jnp.float32) * (2.0 * math.pi / width)
    return (jnp.cos(angle).astype(jnp.bfloat16), jnp.sin(angle).astype(jnp.bfloat16))

def on_left(table, values):
    return jnp.einsum('kn,mnj->mkj', table.astype(jnp.float32), values.astype(jnp.float32))

def on_right(values, table):
    return jnp.einsum('mkn,nj->mkj', values.astype(jnp.float32), table.astype(jnp.float32))

def scan_terms(probe_real, probe_imag, patch, amplitude, cosine, sine, width):
    patch_real = patch[0]
    patch_imag = patch[1]
    psi_real = (probe_real * patch_real - probe_imag * patch_imag).astype(jnp.bfloat16)
    psi_imag = (probe_real * patch_imag + probe_imag * patch_real).astype(jnp.bfloat16)
    left_real = (on_left(cosine, psi_real) + on_left(sine, psi_imag)).astype(jnp.bfloat16)
    left_imag = (on_left(cosine, psi_imag) - on_left(sine, psi_real)).astype(jnp.bfloat16)
    far_real = (on_right(left_real, cosine) + on_right(left_imag, sine)) / width
    far_imag = (on_right(left_imag, cosine) - on_right(left_real, sine)) / width
    inten = lax.optimization_barrier(jnp.sum(far_real * far_real + far_imag * far_imag, axis=0))
    factor = 1.0 - amplitude / jnp.sqrt(inten + floor_term)
    chi_real = (far_real * factor).astype(jnp.bfloat16)
    chi_imag = (far_imag * factor).astype(jnp.bfloat16)
    back_real = (on_left(cosine, chi_real) - on_left(sine, chi_imag)).astype(jnp.bfloat16)
    back_imag = (on_left(cosine, chi_imag) + on_left(sine, chi_real)).astype(jnp.bfloat16)
    grad_real = (on_right(back_real, cosine) - on_right(back_imag, sine)) / width
    grad_imag = (on_right(back_imag, cosine) + on_right(back_real, sine)) / width
    patch_grad = jnp.stack([lax.optimization_barrier(jnp.sum(probe_real * grad_real + probe_imag * grad_imag, axis=0)), lax.optimization_barrier(jnp.sum(probe_real * grad_imag - probe_imag * grad_real, axis=0))])
    probe_term = jnp.stack([patch_real * grad_real + patch_imag * grad_imag, patch_real * grad_imag - patch_imag * grad_real], axis=1)
    return (patch_grad, probe_term)

def reference(field, probe, amplitudes, offsets, counts):
    half = P_SIZE // 2
    padded = jnp.pad(field, ((0, 0), (half, half), (half, half)))
    cosine, sine = dft_tables(P_SIZE)
    probe_real = probe[:, 0].astype(jnp.float32)
    probe_imag = probe[:, 1].astype(jnp.float32)
    total = N_XT * N_YT * SLOTS
    flat = jnp.arange(total, dtype=jnp.int32)
    tile_row = flat // (N_YT * SLOTS)
    tile_col = flat // SLOTS % N_YT
    slot_index = flat % SLOTS
    zero_index = jnp.zeros((), jnp.int32)

    def visit(carry, entry):
        grad_pad, probe_grad = carry
        row, col, slot = entry
        anchor_row = (row * TILE + offsets[row, col, slot, 0]).astype(jnp.int32)
        anchor_col = (col * TILE + offsets[row, col, slot, 1]).astype(jnp.int32)
        patch = lax.dynamic_slice(padded, (zero_index, anchor_row, anchor_col), (2, P_SIZE, P_SIZE))
        amplitude = amplitudes[row, col, slot].astype(jnp.float32)
        patch_grad, probe_term = scan_terms(probe_real, probe_imag, patch, amplitude, cosine, sine, P_SIZE)
        weight = (slot < counts[row, col]).astype(jnp.float32)
        current = lax.dynamic_slice(grad_pad, (zero_index, anchor_row, anchor_col), (2, P_SIZE, P_SIZE))
        grad_pad = lax.dynamic_update_slice(grad_pad, current + weight * patch_grad, (zero_index, anchor_row, anchor_col))
        probe_grad = probe_grad + weight * probe_term
        return ((grad_pad, probe_grad), None)
    start = (jnp.zeros(padded.shape, jnp.float32), jnp.zeros((MODES, 2, P_SIZE, P_SIZE), jnp.float32))
    (grad_pad, probe_grad), _ = lax.scan(visit, start, (tile_row, tile_col, slot_index))
    field_grad = grad_pad[:, half:half + OX, half:half + OY]
    new_field = field - field_rate * field_grad
    new_probe = probe.astype(jnp.float32) - probe_rate * probe_grad
    return (new_field, new_probe)
```

```python
import math

import numpy as np
import ml_dtypes
import jax
import jax.numpy as jnp
from jax import lax
from jax.experimental import pallas as pl
from jax.experimental.pallas import tpu as pltpu
from jax.sharding import PartitionSpec as P

floor_term = 0.5
field_rate = 0.25
probe_rate = 0.1
grid_axes = ("xt", "yt", "sg")


def half_spectrum_order(width):
    half = width // 2
    return np.concatenate([np.arange(half), [half], np.arange(width - 1, half, -1)])


def real_tables(width):
    half = width // 2
    index = np.arange(width)
    angle = (index[:, None] * index[None, :] % width) * (2.0 * math.pi / width)
    cosine, sine = np.cos(angle), np.sin(angle)
    cosine[np.abs(cosine) < 1e-9] = 0.0
    rows = np.concatenate([cosine[: half + 1], sine[1:half]], axis=0)
    select = np.eye(width)[half_spectrum_order(width)]
    return [np.asarray(x, dtype=ml_dtypes.bfloat16) for x in (rows, rows.T, select, select.T)]


def dot(a, b):
    return jnp.dot(a, b, preferred_element_type=jnp.float32)


def scan_kernel(meta_ref, offs_ref, tile_ref, mine_ref, other_ref, probe_ref, amp_ref, rows_ref, cols_ref,
                sel_ref, selt_ref, keep_grad_ref, send_grad_ref, keep_probe_ref, send_probe_ref,
                pad_ref, grad_ref, pg_ref, patch_ref, far_ref, acc_ref, fac_ref):
    modes = probe_ref.shape[0]
    width = probe_ref.shape[-1]
    half = width // 2
    bf16 = jnp.bfloat16
    grad_ref[...] = jnp.zeros_like(grad_ref)
    core = meta_ref[1]
    side = meta_ref[2]
    middle = 1 - core
    for j in range(2):
        for i in range(2):
            pad_ref[:, 1 + j, (1 + i) * half : (2 + i) * half] = tile_ref[:, i * half : (i + 1) * half, j * half : (j + 1) * half]
    for source, at in ((mine_ref, core), (other_ref, middle)):
        margin = pl.ds(pl.multiple_of(at * 3 * half, half), half)
        strip = pl.ds(pl.multiple_of((at + 1) * half, half), half)
        pad_ref[:, 1, margin] = source[:, :, :half]
        pad_ref[:, 2, margin] = source[:, :, half:width]
        for step in range(2):
            block = side if step == 0 else 3 - side
            start = width + step * width
            if start < source.shape[-1]:
                pad_ref[:, block, strip] = source[:, :, start : start + half]
                pad_ref[:, block, margin] = source[:, :, start + half : start + width]
            else:
                pad_ref[:, block, strip] = jnp.zeros((2, half, half), jnp.float32)
                pad_ref[:, block, margin] = jnp.zeros((2, half, half), jnp.float32)
    pg_ref[...] = jnp.zeros_like(pg_ref)
    row_zero = lax.broadcasted_iota(jnp.int32, (half, width), 0) == 0
    col_zero = lax.broadcasted_iota(jnp.int32, (width, half), 1) == 0

    def split(re, im, axis):
        zero = row_zero if axis == 0 else col_zero
        cut = (lambda x: (x[:half], x[half:])) if axis == 0 else (lambda x: (x[:, :half], x[:, half:]))
        ar, br = cut(re)
        ai, bi = cut(im)
        bi0 = jnp.where(zero, 0.0, bi)
        br0 = jnp.where(zero, 0.0, br)
        lr, li = ar + bi0, ai - br0
        hr = jnp.where(zero, br, ar - bi)
        hi = jnp.where(zero, bi, ai + br)
        return jnp.concatenate([lr, hr], axis), jnp.concatenate([li, hi], axis)

    def fold(re, im, axis):
        zero = row_zero if axis == 0 else col_zero
        cut = (lambda x: (x[:half], x[half:])) if axis == 0 else (lambda x: (x[:, :half], x[:, half:]))
        r1, r2 = cut(re)
        i1, i2 = cut(im)
        lr = r1 + jnp.where(zero, 0.0, r2)
        li = i1 + jnp.where(zero, 0.0, i2)
        hr = jnp.where(zero, r2, i2 - i1)
        hi = jnp.where(zero, i2, r1 - r2)
        return (jnp.concatenate([lr, hr], axis).astype(bf16), jnp.concatenate([li, hi], axis).astype(bf16))

    def visit(s, carry):
        row = offs_ref[s, 0]
        col = offs_ref[s, 1]
        base = jnp.where(col >= half, 1, 0)
        shift = col - base * half
        for comp in range(2):
            win = jnp.concatenate([pad_ref[comp, base + j, pl.ds(row, width), :] for j in range(3)], axis=1)
            win = pltpu.roll(win, lax.rem(width + half - shift, width + half), 1)
            patch_ref[comp] = win[:, :width]
        amp = dot(dot(sel_ref[...], amp_ref[s]).astype(bf16), selt_ref[...])
        fac_ref[...] = jnp.zeros_like(fac_ref)

        def forward(m, carry):
            qr = probe_ref[m, 0].astype(jnp.float32)
            qi = probe_ref[m, 1].astype(jnp.float32)
            pr = patch_ref[0]
            pi = patch_ref[1]
            psi_r = (qr * pr - qi * pi).astype(bf16)
            psi_i = (qr * pi + qi * pr).astype(bf16)
            yr, yi = split(dot(rows_ref[...], psi_r), dot(rows_ref[...], psi_i), 0)
            fr, fi = split(dot(yr.astype(bf16), cols_ref[...]), dot(yi.astype(bf16), cols_ref[...]), 1)
            far_ref[m, 0] = fr
            far_ref[m, 1] = fi
            fac_ref[...] += fr * fr + fi * fi
            return carry

        lax.fori_loop(0, modes, forward, 0, unroll=True)
        scale = 1.0 / (width * width)
        fac_ref[...] = (scale - amp * scale * lax.rsqrt(fac_ref[...] * scale + floor_term))
        acc_ref[...] = jnp.zeros_like(acc_ref)

        def backward(m, carry):
            f = fac_ref[...]
            ur, ui = fold(far_ref[m, 0] * f, far_ref[m, 1] * f, 0)
            vr, vi = fold(dot(cols_ref[...], ur), dot(cols_ref[...], ui), 1)
            gr = dot(vr, rows_ref[...])
            gi = dot(vi, rows_ref[...])
            qr = probe_ref[m, 0].astype(jnp.float32)
            qi = probe_ref[m, 1].astype(jnp.float32)
            pr = patch_ref[0]
            pi = patch_ref[1]
            acc_ref[0] += qr * gr + qi * gi
            acc_ref[1] += qr * gi - qi * gr
            pg_ref[m, 0] += pr * gr + pi * gi
            pg_ref[m, 1] += pr * gi - pi * gr
            return carry

        lax.fori_loop(0, modes, backward, 0, unroll=True)
        for comp in range(2):
            wide = jnp.concatenate([acc_ref[comp], jnp.zeros((width, half), jnp.float32)], axis=1)
            wide = pltpu.roll(wide, shift, 1)
            for j in range(3):
                at = (comp, base + j, pl.ds(row, width), slice(None))
                grad_ref[at] = grad_ref[at] + wide[:, j * half : (j + 1) * half]
        return carry

    lax.fori_loop(0, meta_ref[0], visit, 0)
    for target, at in ((keep_grad_ref, core), (send_grad_ref, middle)):
        main = pl.ds(pl.multiple_of((at + 1) * half, half), half)
        margin = pl.ds(pl.multiple_of((1 - at) * 3 * half, half), half)
        target[0] = grad_ref[:, :, main]
        target[1] = grad_ref[:, :, margin]
    share = modes // 2
    keep_probe_ref[...] = pg_ref[pl.ds(core * share, share)]
    send_probe_ref[...] = pg_ref[pl.ds(middle * share, share)]


def scans(meta, offs, tile, mine, other, probe, amp):
    modes, _, width, _ = probe.shape
    half = width // 2
    tables = [jnp.asarray(t) for t in real_tables(width)]
    smem = pl.BlockSpec(memory_space=pltpu.SMEM)
    vmem = pl.BlockSpec(memory_space=pltpu.VMEM)
    grad = jax.ShapeDtypeStruct((2, 2, 4, half, half), jnp.float32)
    share = jax.ShapeDtypeStruct((modes // 2, 2, width, width), jnp.float32)
    return pl.pallas_call(
        scan_kernel,
        out_shape=(grad, grad, share, share),
        in_specs=[smem, smem] + [vmem] * 9,
        out_specs=(vmem,) * 4,
        scratch_shapes=[
            pltpu.VMEM((2, 4, 2 * width, half), jnp.float32),
            pltpu.VMEM((2, 4, 2 * width, half), jnp.float32),
            pltpu.VMEM((modes, 2, width, width), jnp.float32),
            pltpu.VMEM((2, width, width), jnp.float32),
            pltpu.VMEM((modes, 2, width, width), jnp.float32),
            pltpu.VMEM((2, width, width), jnp.float32),
            pltpu.VMEM((width, width), jnp.float32),
        ],
        compiler_params=pltpu.CompilerParams(vmem_limit_bytes=40 * 2**20),
        cost_estimate=pl.CostEstimate(flops=4 * 10**9, bytes_accessed=8 * 2**20, transcendentals=0),
    )(meta, offs, tile, mine, other, probe, amp, *tables)


def route(target):
    rows, cols, cores = (lax.axis_size(a) for a in grid_axes)
    pairs = []
    for z in range(rows):
        for x in range(cols):
            for c in range(cores):
                to = target(z, x, c)
                if to is not None and 0 <= to[0] < rows and 0 <= to[1] < cols:
                    pairs.append(((z * cols + x) * cores + c, (to[0] * cols + to[1]) * cores + to[2]))
    return pairs


def move(block, target):
    return lax.ppermute(block, grid_axes, route(target))


def across(x, step):
    return x + 1 if x % 2 == step else x - 1


def down(z, c):
    return z + 1 if c == 0 else z - 1


def swap_cores(block):
    return move(block, lambda z, x, c: (z, x, 1 - c))


def axis_bits(axis):
    return [(axis, b) for b in range(lax.axis_size(axis).bit_length() - 1)]


def reduce_orders():
    first, second = axis_bits("yt"), axis_bits("xt")
    a, b = [], []
    for i in range(max(len(first), len(second))):
        pair = first[i : i + 1] + second[i : i + 1]
        a += pair
        b += pair[::-1]
    return list(zip(a, b))


def flip(order):
    def target(z, x, c):
        axis, bit = order[c]
        return (z ^ (1 << bit), x, c) if axis == "xt" else (z, x ^ (1 << bit), c)

    return target


def bit_of(order, core):
    bits = [(lax.axis_index(axis) >> bit) & 1 for axis, bit in order]
    return jnp.where(core == 0, bits[0], bits[1])


def pick(block, index):
    return lax.dynamic_index_in_dim(block, index, 0, keepdims=False)


def joined(own, other, bit):
    return jnp.where(bit == 0, jnp.concatenate([own, other], 0), jnp.concatenate([other, own], 0))


def new_probe_share(part, probe_part, core):
    orders = reduce_orders()
    shape = part.shape
    part = part.reshape(-1, shape[-1])
    probe_part = probe_part.reshape(-1, shape[-1])
    for order in orders[:-1]:
        bit = bit_of(order, core)
        part = part.reshape(2, -1, shape[-1])
        got = move(pick(part, 1 - bit), flip(order))
        part = pick(part, bit) + got
        probe_part = pick(probe_part.reshape(2, -1, shape[-1]), bit)
    for order in orders[-1:]:
        part = part + move(part, flip(order))
    part = probe_part.astype(jnp.float32) - probe_rate * part
    for order in orders[:-1][::-1]:
        part = joined(part, move(part, flip(order)), bit_of(order, core))
    return part.reshape(shape)


def shards(field, probe, amplitudes, offsets, counts):
    modes, _, width, _ = probe.shape
    half = width // 2
    per_device = amplitudes.shape[2]
    core = lax.axis_index("sg")
    odd = lax.axis_index("yt") % 2
    steps = min(2, lax.axis_size("yt") - 1)
    live = jnp.clip(counts[0, 0] - core * per_device, 0, per_device)
    side = jnp.where(odd == 0, 3, 0)
    meta = jnp.stack([live, core, side]).astype(jnp.int32)

    outer = lax.dynamic_slice_in_dim(field, (1 - core) * half, half, 1)
    inner = lax.dynamic_slice_in_dim(field, core * half, half, 1)
    parts = [move(outer, lambda z, x, c: (down(z, c), x, c))]
    for step in range(steps):
        start = jnp.where(odd == step, half, 0)
        parts.append(move(lax.dynamic_slice_in_dim(inner, start, half, 2), lambda z, x, c: (z, across(x, step), c)))
        parts.append(move(lax.dynamic_slice_in_dim(outer, start, half, 2), lambda z, x, c: (down(z, c), across(x, step), c)))
    mine = jnp.concatenate(parts, axis=2)
    other = swap_cores(mine)

    keep_grad, send_grad, keep_probe, send_probe = scans(
        meta, offsets[0, 0], field, mine, other, probe, amplitudes[0, 0]
    )

    share = keep_probe + swap_cores(send_probe)
    grad = keep_grad + swap_cores(send_grad)
    main, margin = grad[0], grad[1]
    below = move(margin[:, 1:3], lambda z, x, c: (down(z, c), x, c))
    total = main[:, 1:3] + below
    blocks = [total[:, 0], total[:, 1]]
    for step in range(steps):
        block = jnp.where(odd == step, 3, 0)
        beside = move(lax.dynamic_index_in_dim(main, block, 1, keepdims=False), lambda z, x, c: (z, across(x, step), c))
        corner = move(lax.dynamic_index_in_dim(margin, block, 1, keepdims=False), lambda z, x, c: (down(z, c), across(x, step), c))
        extra = beside + corner
        blocks[0] = blocks[0] + jnp.where(odd == step, 0.0, extra)
        blocks[1] = blocks[1] + jnp.where(odd == step, extra, 0.0)
    new_field = inner - field_rate * jnp.concatenate(blocks, axis=2)

    probe_part = lax.dynamic_slice_in_dim(probe, core * (modes // 2), modes // 2, 0)
    own = new_probe_share(share, probe_part, core)
    new_probe = joined(own, swap_cores(own), core)
    return (new_field, new_probe)


def solution(mesh):
    in_specs = (
        P(None, ("groups", "xt"), "yt"),
        P("groups", None, None, None),
        P(("groups", "xt"), "yt", "sg", None, None),
        P(("groups", "xt"), "yt", "sg", None),
        P(("groups", "xt"), "yt"),
    )
    out_specs = (P(None, ("groups", "xt", "sg"), "yt"), P("groups", None, None, None))
    return jax.shard_map(shards, mesh=mesh, in_specs=in_specs, out_specs=out_specs, check_vma=False)
```

```python
import functools
import math

import jax
import jax.numpy as jnp
from jax import lax
from jax.experimental import pallas as pl
from jax.experimental.pallas import tpu as pltpu
from jax.sharding import PartitionSpec as P

floor_term = 0.5
field_rate = 0.25
probe_rate = 0.1
grid_axes = ("xt", "yt", "sg")


def cosine_of(phase, width):
    phase = phase & (width - 1)
    half = width // 2
    near = jnp.minimum(phase, width - phase)
    quarter = jnp.minimum(near, half - near)
    square = jnp.square(quarter.astype(jnp.float32) * (2.0 * math.pi / width))
    value = jnp.zeros_like(square)
    for power in range(12, -1, -2):
        value = value * square + (-1.0) ** (power // 2) / math.factorial(power)
    return jnp.where(near == quarter, value, -value)


def half_spectrum_table(width, axis):
    half = width // 2
    which = lax.broadcasted_iota(jnp.int32, (width, width), axis)
    other = lax.broadcasted_iota(jnp.int32, (width, width), 1 - axis)
    sine = which > half
    phase = jnp.where(sine, which - half, which) * other + jnp.where(sine, width - width // 4, 0)
    return cosine_of(phase, width).astype(jnp.bfloat16)


def half_spectrum_select(width):
    half = width // 2
    row = lax.broadcasted_iota(jnp.int32, (width, width), 0)
    col = lax.broadcasted_iota(jnp.int32, (width, width), 1)
    return (jnp.where(row > half, width + half - row, row) == col).astype(jnp.float32).astype(jnp.bfloat16)


def dot(a, b):
    return jnp.dot(a, b, preferred_element_type=jnp.float32)


def halves(x, axis):
    cut = x.shape[axis] // 2
    return (x[:cut], x[cut:]) if axis == 0 else (x[:, :cut], x[:, cut:])


def patched(general, special, axis):
    if axis == 0:
        first = lax.broadcasted_iota(jnp.int32, (8, general.shape[1]), 0) == 0
        return jnp.concatenate([jnp.where(first, special[:8], general[:8]), general[8:]], 0)
    first = lax.broadcasted_iota(jnp.int32, general.shape, 1) == 0
    return jnp.where(first, special, general)


def split(re, im, axis):
    ar, br = halves(re, axis)
    ai, bi = halves(im, axis)
    re = jnp.concatenate([patched(ar + bi, ar, axis), patched(ar - bi, br, axis)], axis)
    im = jnp.concatenate([patched(ai - br, ai, axis), patched(ai + br, bi, axis)], axis)
    return re, im


def fold(re, im, axis):
    r1, r2 = halves(re, axis)
    i1, i2 = halves(im, axis)
    re = jnp.concatenate([patched(r1 + r2, r1, axis), patched(i2 - i1, r2, axis)], axis)
    im = jnp.concatenate([patched(i1 + i2, i1, axis), patched(r1 - r2, i2, axis)], axis)
    return re.astype(jnp.bfloat16), im.astype(jnp.bfloat16)


def mode_terms(ur, ui, probe_ref, mode, pr, pi, rows, cols):
    vr, vi = fold(dot(cols, ur), dot(cols, ui), 1)
    g = dot(jnp.concatenate([vr, vi], 0), rows)
    gr, gi = g[: g.shape[0] // 2], g[g.shape[0] // 2 :]
    qr = probe_ref[mode, 0].astype(jnp.float32)
    qi = probe_ref[mode, 1].astype(jnp.float32)
    return (
        (qr * gr + qi * gi, qr * gi - qi * gr),
        (pr * gr + pi * gi, pr * gi - pi * gr),
    )


def place_shares(meta_ref, probe_ref, pg_ref, keep_ref, send_ref, chunk, blocks):
    core, mode_bits, other_bits, base = (meta_ref[i] for i in (1, 3, 4, 5))
    modes, _, width, _ = probe_ref.shape
    share = modes // 2
    part = share // 2
    size = part * 2 * width // blocks
    starting = jnp.where(base == 1, 1.0, 0.0)

    def place(p, carry):
        here = pl.ds(pl.multiple_of(p * size, size), size)
        for target, at, bits, own in ((keep_ref, core, mode_bits, True), (send_ref, 1 - core, other_bits, False)):
            line = (p ^ bits) * size
            first = line // (2 * width)
            comp = line % (2 * width) // width
            inside = pl.ds(pl.multiple_of(line % width, size), size)
            value = -probe_rate * pg_ref[at * part + first, comp, inside]
            if own:
                value += starting * probe_ref[at * share + chunk * part + first, comp, inside].astype(jnp.float32)
            target[here] = value
        return carry

    lax.fori_loop(0, blocks, place, 0, unroll=blocks <= 8)


def chunk_modes(modes, chunk):
    part = modes // 4
    return [core * 2 * part + chunk * part + i for core in range(2) for i in range(part)]


def first_kernel(blocks, meta_ref, offs_ref, tile_ref, mine_ref, other_ref, probe_ref, amp_ref, table_ref,
                 keep_ref, send_ref, patch_ref, later_ref, acc_ref, pad_ref, far_ref, pg_ref):
    modes, _, width, _ = probe_ref.shape
    half = width // 2
    core, side = meta_ref[1], meta_ref[2]
    for source, at in ((mine_ref, core), (other_ref, 1 - core)):
        margin = pl.ds(pl.multiple_of(at * 3 * half, half), half)
        strip = pl.ds(pl.multiple_of((at + 1) * half, half), half)
        pad_ref[:, 1, margin] = source[:, :, :half]
        pad_ref[:, 2, margin] = source[:, :, half:width]
        for step in range(2):
            block = side if step == 0 else 3 - side
            start = width + step * width
            if start < source.shape[-1]:
                pad_ref[:, block, strip] = source[:, :, start : start + half]
                pad_ref[:, block, margin] = source[:, :, start + half : start + width]
            else:
                pad_ref[:, block, strip] = jnp.zeros((2, half, half), jnp.float32)
                pad_ref[:, block, margin] = jnp.zeros((2, half, half), jnp.float32)
    for j in range(2):
        pad_ref[:, 1 + j, half : half + width] = tile_ref[:, :, j * half : (j + 1) * half]
    pg_ref[...] = jnp.zeros_like(pg_ref)
    rows, cols = table_ref[0], table_ref[1]
    now, later = chunk_modes(modes, 0), chunk_modes(modes, 1)

    def visit(s, carry):
        row = offs_ref[0, s]
        col = offs_ref[1, s]
        block = jnp.where(col >= half, 1, 0)
        shift = col - block * half
        for comp in range(2):
            win = jnp.concatenate([pad_ref[comp, block + j, pl.ds(row, width), :] for j in range(3)], axis=1)
            patch_ref[s, comp] = pltpu.roll(win, lax.rem(width + half - shift, width + half), 1)[:, :width]
        inten = None
        for m in range(modes):
            qr = probe_ref[m, 0].astype(jnp.float32)
            qi = probe_ref[m, 1].astype(jnp.float32)
            pr = patch_ref[s, 0]
            pi = patch_ref[s, 1]
            psi_r = (qr * pr - qi * pi).astype(jnp.bfloat16)
            psi_i = (qr * pi + qi * pr).astype(jnp.bfloat16)
            yr, yi = split(dot(rows, psi_r), dot(rows, psi_i), 0)
            y = dot(jnp.concatenate([yr, yi], 0).astype(jnp.bfloat16), cols)
            fr, fi = split(y[:width], y[width:], 1)
            far_ref[m, 0] = fr
            far_ref[m, 1] = fi
            power = fr * fr + fi * fi
            inten = power if inten is None else inten + power
        scale = 1.0 / (width * width)
        factor = scale - amp_ref[s] * scale * lax.rsqrt(inten * scale + floor_term)
        total = None
        for m in now:
            ur, ui = fold(far_ref[m, 0] * factor, far_ref[m, 1] * factor, 0)
            at, term = mode_terms(ur, ui, probe_ref, m, patch_ref[s, 0], patch_ref[s, 1], rows, cols)
            total = at if total is None else (total[0] + at[0], total[1] + at[1])
            for comp in range(2):
                pg_ref[now.index(m), comp] += term[comp]
        for comp in range(2):
            acc_ref[s, comp] = total[comp]
        for m in later:
            ur, ui = fold(far_ref[m, 0] * factor, far_ref[m, 1] * factor, 0)
            later_ref[s, later.index(m), 0] = ur
            later_ref[s, later.index(m), 1] = ui
        return carry

    lax.fori_loop(0, meta_ref[0], visit, 0)
    place_shares(meta_ref, probe_ref, pg_ref, keep_ref, send_ref, 0, blocks)


def second_kernel(blocks, meta_ref, offs_ref, tile_ref, probe_ref, table_ref, patch_ref, later_ref, acc_ref,
                  keep_ref, send_ref, keep_grad_ref, send_grad_ref, grad_ref, pg_ref):
    modes, _, width, _ = probe_ref.shape
    half = width // 2
    core = meta_ref[1]
    grad_ref[...] = jnp.zeros_like(grad_ref)
    pg_ref[...] = jnp.zeros_like(pg_ref)
    rows, cols = table_ref[0], table_ref[1]
    later = chunk_modes(modes, 1)

    def visit(s, carry):
        row = offs_ref[0, s]
        col = offs_ref[1, s]
        block = jnp.where(col >= half, 1, 0)
        shift = col - block * half
        total = (acc_ref[s, 0], acc_ref[s, 1])
        for i, m in enumerate(later):
            at, term = mode_terms(later_ref[s, i, 0], later_ref[s, i, 1], probe_ref, m,
                                  patch_ref[s, 0], patch_ref[s, 1], rows, cols)
            total = (total[0] + at[0], total[1] + at[1])
            for comp in range(2):
                pg_ref[i, comp] += term[comp]
        for comp in range(2):
            wide = jnp.concatenate([total[comp], jnp.zeros((width, half), jnp.float32)], axis=1)
            wide = pltpu.roll(wide, shift, 1)
            for j in range(3):
                at = (comp, block + j, pl.ds(row, width), slice(None))
                grad_ref[at] = grad_ref[at] + wide[:, j * half : (j + 1) * half]
        return carry

    lax.fori_loop(0, meta_ref[0], visit, 0)
    place_shares(meta_ref, probe_ref, pg_ref, keep_ref, send_ref, 1, blocks)
    for target, at in ((keep_grad_ref, core), (send_grad_ref, 1 - core)):
        main = pl.ds(pl.multiple_of((at + 1) * half, half), half)
        margin = pl.ds(pl.multiple_of((1 - at) * 3 * half, half), half)
        target[0] = -field_rate * grad_ref[:, :, main]
        target[1] = -field_rate * grad_ref[:, :, margin]
    inner = pl.ds(pl.multiple_of(core * half, half), half)
    for j in range(2):
        keep_grad_ref[0, :, 1 + j] += tile_ref[:, inner, j * half : (j + 1) * half]


def prepare(probe, amp):
    width = probe.shape[-1]

    def body(probe_hbm, amp_hbm, probe_ref, amp_ref, table_ref, raw_ref, sems):
        copies = [
            pltpu.make_async_copy(source, target, sems.at[i])
            for i, (source, target) in enumerate([(amp_hbm, raw_ref), (probe_hbm, probe_ref)])
        ]
        for copy in copies:
            copy.start()
        for axis in range(2):
            table_ref[axis] = half_spectrum_table(width, axis)
        select = half_spectrum_select(width)
        copies[0].wait()

        def order(s, carry):
            amp_ref[s] = dot(dot(select, raw_ref[s]).astype(jnp.bfloat16), select)
            return carry

        lax.fori_loop(0, raw_ref.shape[0], order, 0)
        copies[1].wait()

    vmem = pl.BlockSpec(memory_space=pltpu.VMEM)
    hbm = pl.BlockSpec(memory_space=pl.ANY)
    return pl.pallas_call(
        body,
        out_shape=(
            jax.ShapeDtypeStruct(probe.shape, jnp.bfloat16),
            jax.ShapeDtypeStruct(amp.shape, jnp.float32),
            jax.ShapeDtypeStruct((2, width, width), jnp.bfloat16),
        ),
        in_specs=[hbm] * 2,
        out_specs=(vmem,) * 3,
        scratch_shapes=[
            pltpu.VMEM(amp.shape, jnp.bfloat16),
            pltpu.SemaphoreType.DMA((2,)),
        ],
        compiler_params=pltpu.CompilerParams(vmem_limit_bytes=51 * 2**20),
        cost_estimate=pl.CostEstimate(flops=2 * 10**8, bytes_accessed=4 * 2**20, transcendentals=0),
    )(probe, amp)


def first_scans(blocks, meta, offs, tile, mine, other, probe, amp, tables):
    modes, _, width, _ = probe.shape
    half = width // 2
    slots = amp.shape[0]
    part = modes // 4
    smem = pl.BlockSpec(memory_space=pltpu.SMEM)
    vmem = pl.BlockSpec(memory_space=pltpu.VMEM)
    share = jax.ShapeDtypeStruct((part * 2 * width, width), jnp.float32)
    image = jax.ShapeDtypeStruct((slots, 2, width, width), jnp.float32)
    return pl.pallas_call(
        functools.partial(first_kernel, blocks),
        out_shape=(share, share, image, jax.ShapeDtypeStruct((slots, 2 * part, 2, width, width), jnp.bfloat16), image),
        in_specs=[smem] * 2 + [vmem] * 6,
        out_specs=(vmem,) * 5,
        scratch_shapes=[
            pltpu.VMEM((2, 4, 2 * width, half), jnp.float32),
            pltpu.VMEM((modes, 2, width, width), jnp.float32),
            pltpu.VMEM((2 * part, 2, width, width), jnp.float32),
        ],
        compiler_params=pltpu.CompilerParams(vmem_limit_bytes=24 * 2**20),
        cost_estimate=pl.CostEstimate(flops=4 * 10**9, bytes_accessed=8 * 2**20, transcendentals=0),
    )(meta, offs, tile, mine, other, probe, amp, tables)


def second_scans(blocks, meta, offs, tile, probe, tables, patch, later, acc):
    modes, _, width, _ = probe.shape
    half = width // 2
    part = modes // 4
    smem = pl.BlockSpec(memory_space=pltpu.SMEM)
    vmem = pl.BlockSpec(memory_space=pltpu.VMEM)
    grad = jax.ShapeDtypeStruct((2, 2, 4, half, half), jnp.float32)
    share = jax.ShapeDtypeStruct((part * 2 * width, width), jnp.float32)
    return pl.pallas_call(
        functools.partial(second_kernel, blocks),
        out_shape=(share, share, grad, grad),
        in_specs=[smem] * 2 + [vmem] * 6,
        out_specs=(vmem,) * 4,
        scratch_shapes=[
            pltpu.VMEM((2, 4, 2 * width, half), jnp.float32),
            pltpu.VMEM((2 * part, 2, width, width), jnp.float32),
        ],
        compiler_params=pltpu.CompilerParams(vmem_limit_bytes=24 * 2**20),
        cost_estimate=pl.CostEstimate(flops=2 * 10**9, bytes_accessed=8 * 2**20, transcendentals=0),
    )(meta, offs, tile, probe, tables, patch, later, acc)


def route(target):
    rows, cols, cores = (lax.axis_size(a) for a in grid_axes)
    pairs = []
    for z in range(rows):
        for x in range(cols):
            for c in range(cores):
                to = target(z, x, c)
                if to is not None and 0 <= to[0] < rows and 0 <= to[1] < cols:
                    pairs.append(((z * cols + x) * cores + c, (to[0] * cols + to[1]) * cores + to[2]))
    return pairs


def move(block, target):
    return lax.ppermute(block, grid_axes, route(target))


def across(x, step):
    return x + 1 if x % 2 == step else x - 1


def down(z, c):
    return z + 1 if c == 0 else z - 1


def swap_cores(block):
    return move(block, lambda z, x, c: (z, x, 1 - c))


def axis_bits(axis):
    return [(axis, b) for b in range(lax.axis_size(axis).bit_length() - 1)]


def reduce_orders():
    first, second = axis_bits("yt"), axis_bits("xt")
    a, b = [], []
    for i in range(max(len(first), len(second))):
        pair = first[i : i + 1] + second[i : i + 1]
        a += pair
        b += pair[::-1]
    return list(zip(a, b))


def flip(order):
    def target(z, x, c):
        axis, bit = order[c]
        return (z ^ (1 << bit), x, c) if axis == "xt" else (z, x ^ (1 << bit), c)

    return target


def bits_of(orders, core):
    total = 0
    for order in orders:
        bits = [(lax.axis_index(axis) >> bit) & 1 for axis, bit in order]
        total = total * 2 + jnp.where(core == 0, bits[0], bits[1])
    return total


def small_call(body, outs, args, meta=None):
    vmem = pl.BlockSpec(memory_space=pltpu.VMEM)
    extra = [] if meta is None else [meta]
    return pl.pallas_call(
        body,
        out_shape=tuple(jax.ShapeDtypeStruct(shape, jnp.float32) for shape in outs),
        in_specs=[pl.BlockSpec(memory_space=pltpu.SMEM)] * len(extra) + [vmem] * len(args),
        out_specs=(vmem,) * len(outs),
        compiler_params=pltpu.CompilerParams(vmem_limit_bytes=6 * 2**20),
        cost_estimate=pl.CostEstimate(flops=10**6, bytes_accessed=2**20, transcendentals=0),
    )(*extra, *args)


def add_split(own, got):
    rows, lanes = own.shape
    cut = rows // 2

    def body(a, b, low, high):
        high[...] = a[cut:] + b[cut:]
        low[...] = a[:cut] + b[:cut]

    return small_call(body, [(cut, lanes)] * 2, [own, got])


def add(own, got):
    def body(a, b, out):
        out[...] = a[...] + b[...]

    return small_call(body, [own.shape], [own, got])[0]


def stack(own, got):
    rows, lanes = own.shape

    def body(a, b, out):
        out[:rows] = a[...]
        out[rows:] = b[...]

    return small_call(body, [(2 * rows, lanes)], [own, got])[0]


def strips(field, meta, steps):
    _, tile, width = field.shape
    half = width // 2

    def body(meta_ref, tile_ref, outer_ref, *refs):
        sems = refs[-1]
        core, odd = meta_ref[0], meta_ref[1]
        outer = pl.ds(pl.multiple_of((1 - core) * half, half), half)
        inner = pl.ds(pl.multiple_of(core * half, half), half)
        copies = [pltpu.make_async_copy(tile_ref.at[:, outer], outer_ref, sems.at[0])]
        for step in range(steps):
            at = odd if step == 1 else 1 - odd
            cols = pl.ds(pl.multiple_of(at * half, half), half)
            for i, rows in enumerate((inner, outer)):
                n = 2 * step + i
                copies.append(pltpu.make_async_copy(tile_ref.at[:, rows, cols], refs[n], sems.at[1 + n]))
        for copy in copies:
            copy.start()
        for copy in copies:
            copy.wait()

    vmem = pl.BlockSpec(memory_space=pltpu.VMEM)
    shapes = [(2, half, width)] + [(2, half, half)] * (2 * steps)
    return pl.pallas_call(
        body,
        out_shape=tuple(jax.ShapeDtypeStruct(shape, jnp.float32) for shape in shapes),
        in_specs=[pl.BlockSpec(memory_space=pltpu.SMEM), pl.BlockSpec(memory_space=pl.ANY)],
        out_specs=(vmem,) * len(shapes),
        scratch_shapes=[pltpu.SemaphoreType.DMA((1 + 2 * steps,))],
        compiler_params=pltpu.CompilerParams(vmem_limit_bytes=6 * 2**20),
        cost_estimate=pl.CostEstimate(flops=10**6, bytes_accessed=2**20, transcendentals=0),
    )(meta, field)


def fold_sends(keep, got, meta, steps):
    half = keep.shape[-1]

    def body(meta_ref, a, b, *refs):
        mid_ref, refs = refs[-1], refs[:-1]
        for step in range(steps):
            block = meta_ref[2] if step == 0 else 3 - meta_ref[2]
            refs[step][...] = a[:, :, block] + b[:, :, block]
        mid_ref[...] = a[:, :, 1:3] + b[:, :, 1:3]

    shapes = [(2, 2, half, half)] * steps + [(2, 2, 2, half, half)]
    *edges, mid = small_call(body, shapes, [keep, got], meta)
    return edges, mid


def fold_join(mid, arrived, meta):
    half = mid.shape[-1]

    def body(meta_ref, mid_ref, *refs):
        down_ref, main_ref = refs[-2:]
        for j in range(2):
            total = mid_ref[:, :, j]
            for step, ref in enumerate(refs[:-2]):
                total += jnp.where((meta_ref[6] + step + j) % 2 == 1, 1.0, 0.0) * ref[...]
            main_ref[:, j] = total[0]
            down_ref[:, j] = total[1]

    return small_call(body, [(2, 2, half, half)] * 2, [mid, *arrived], meta)


def fold_finish(main, below):
    half = main.shape[-1]

    def body(main_ref, below_ref, out_ref):
        for j in range(2):
            out_ref[:, :, j * half : (j + 1) * half] = main_ref[:, j] + below_ref[:, j]

    return small_call(body, [(2, half, 2 * half)], [main, below])[0]


def place_probe(chunks, meta, blocks, shape, sibling, into=None):
    modes, _, width, _ = shape
    share = modes // 2
    part = share // 2
    size = part * 2 * width // blocks
    given = [] if into is None else [into]

    def body(meta_ref, *refs):
        sem = refs[-1]
        out_ref = refs[-2]
        at = 1 - meta_ref[1] if sibling else meta_ref[1]
        bits = meta_ref[4] if sibling else meta_ref[3]

        def copies(p):
            found = []
            for k in range(2):
                line = ((at * share + k * part) * 2 * width) + (p ^ bits) * size
                target = out_ref.at[line // (2 * width), line % (2 * width) // width,
                                    pl.ds(pl.multiple_of(line % width, size), size)]
                here = refs[k].at[pl.ds(pl.multiple_of(p * size, size), size)]
                found.append(pltpu.make_async_copy(here, target, sem.at[p, k]))
            return found

        def start(p, carry):
            for copy in copies(p):
                copy.start()
            return carry

        def wait(p, carry):
            for copy in copies(p):
                copy.wait()
            return carry

        lax.fori_loop(0, blocks, start, 0)
        lax.fori_loop(0, blocks, wait, 0)

    anywhere = pl.BlockSpec(memory_space=pl.ANY)
    return pl.pallas_call(
        body,
        out_shape=jax.ShapeDtypeStruct(shape, jnp.float32),
        in_specs=[pl.BlockSpec(memory_space=pltpu.SMEM)] + [anywhere] * (2 + len(given)),
        out_specs=anywhere,
        input_output_aliases={3: 0} if given else {},
        scratch_shapes=[pltpu.SemaphoreType.DMA((blocks, 2))],
        compiler_params=pltpu.CompilerParams(vmem_limit_bytes=6 * 2**20),
        cost_estimate=pl.CostEstimate(flops=10**6, bytes_accessed=2**21, transcendentals=0),
    )(meta, *chunks, *given)


def shards(field, probe, amplitudes, offsets, counts):
    modes, _, width, _ = probe.shape
    per_device = amplitudes.shape[2]
    core = lax.axis_index("sg")
    odd = lax.axis_index("yt") % 2
    steps = min(2, lax.axis_size("yt") - 1)
    orders = reduce_orders()
    early, last = orders[:-1], orders[-1]
    blocks = 2 ** len(early)
    live = jnp.clip(counts[0, 0] - core * per_device, 0, per_device)
    side = jnp.where(odd == 0, 3, 0)
    base = jnp.where((lax.axis_index("xt") == 0) & (lax.axis_index("yt") == 0), 1, 0)
    meta = jnp.stack(
        [live, core, side, bits_of(early, core), bits_of(early, 1 - core), base, odd]
    ).astype(jnp.int32)
    offs = offsets[0, 0].T
    place = jnp.stack([core, odd]).astype(jnp.int32)

    outer, *edges = strips(field, place, steps)
    prepared = prepare(probe, amplitudes[0, 0])
    parts = [move(outer, lambda z, x, c: (down(z, c), x, c))]
    for step in range(steps):
        parts.append(move(edges[2 * step], lambda z, x, c: (z, across(x, step), c)))
        parts.append(move(edges[2 * step + 1], lambda z, x, c: (down(z, c), across(x, step), c)))
    parts, prepared, meta = lax.optimization_barrier((parts, prepared, meta))
    mine = jnp.concatenate(parts, axis=2)
    other = swap_cores(mine)

    probe_now, amp_now, tables = prepared
    keep, send, *kept = first_scans(blocks, meta, offs, field, mine, other, probe_now, amp_now, tables)
    second = second_scans(blocks, meta, offs, field, probe_now, tables, *kept)
    received, second = lax.optimization_barrier((swap_cores(send), second))
    keep2, send2, keep_grad, send_grad = second
    pairs = [add_split(keep, received), add_split(keep2, swap_cores(send2))]
    got = [move(high, flip(early[0])) for _, high in pairs]
    edges, mid = fold_sends(keep_grad, swap_cores(send_grad), meta, steps)
    arrived = [
        move(edge, lambda z, x, c, step=step: (z, across(x, step), c)) for step, edge in enumerate(edges)
    ]
    for order in early[1:]:
        pairs = [add_split(low, g) for (low, _), g in zip(pairs, got)]
        got = [move(high, flip(order)) for _, high in pairs]
    parts = [add(low, g) for (low, _), g in zip(pairs, got)]
    parts = [add(p, move(p, flip(last))) for p in parts]
    parts[1], arrived = lax.optimization_barrier((parts[1], arrived))
    down_part, main = fold_join(mid, arrived, meta)
    below = move(down_part, lambda z, x, c: (down(z, c), x, c))
    for order in early[::-1]:
        parts = [stack(p, move(p, flip(order))) for p in parts]
    parts[0], below = lax.optimization_barrier((parts[0], below))
    new_field = fold_finish(main, below)
    theirs = [swap_cores(p) for p in parts]
    new_probe = place_probe(parts, meta, blocks, probe.shape, False)
    new_probe = place_probe(theirs, meta, blocks, probe.shape, True, new_probe)
    return (new_field, new_probe)


def solution(mesh):
    in_specs = (
        P(None, ("groups", "xt"), "yt"),
        P("groups", None, None, None),
        P(("groups", "xt"), "yt", "sg", None, None),
        P(("groups", "xt"), "yt", "sg", None),
        P(("groups", "xt"), "yt"),
    )
    out_specs = (P(None, ("groups", "xt", "sg"), "yt"), P("groups", None, None, None))
    return jax.shard_map(shards, mesh=mesh, in_specs=in_specs, out_specs=out_specs, check_vma=False)
```

```python
import functools
import math

import jax
import jax.numpy as jnp
from jax import lax
from jax.experimental import pallas as pl
from jax.experimental.pallas import tpu as pltpu
from jax.sharding import PartitionSpec as P

floor_term = 0.5
field_rate = 0.25
probe_rate = 0.1
grid_axes = ("xt", "yt", "sg")


def cosine_of(phase, width):
    phase = phase & (width - 1)
    half = width // 2
    near = jnp.minimum(phase, width - phase)
    quarter = jnp.minimum(near, half - near)
    square = jnp.square(quarter.astype(jnp.float32) * (2.0 * math.pi / width))
    value = jnp.zeros_like(square)
    for power in range(12, -1, -2):
        value = value * square + (-1.0) ** (power // 2) / math.factorial(power)
    return jnp.where(near == quarter, value, -value)


def half_spectrum_table(width, axis):
    half = width // 2
    which = lax.broadcasted_iota(jnp.int32, (width, width), axis)
    other = lax.broadcasted_iota(jnp.int32, (width, width), 1 - axis)
    sine = which > half
    phase = jnp.where(sine, which - half, which) * other + jnp.where(sine, width - width // 4, 0)
    return cosine_of(phase, width).astype(jnp.bfloat16)


def half_spectrum_select(width):
    half = width // 2
    row = lax.broadcasted_iota(jnp.int32, (width, width), 0)
    col = lax.broadcasted_iota(jnp.int32, (width, width), 1)
    return (jnp.where(row > half, width + half - row, row) == col).astype(jnp.float32).astype(jnp.bfloat16)


def dot(a, b):
    return jnp.dot(a, b, preferred_element_type=jnp.float32)


def halves(x, axis):
    cut = x.shape[axis] // 2
    return (x[:cut], x[cut:]) if axis == 0 else (x[:, :cut], x[:, cut:])


def patched(general, special, axis):
    if axis == 0:
        first = lax.broadcasted_iota(jnp.int32, (8, general.shape[1]), 0) == 0
        return jnp.concatenate([jnp.where(first, special[:8], general[:8]), general[8:]], 0)
    first = lax.broadcasted_iota(jnp.int32, general.shape, 1) == 0
    return jnp.where(first, special, general)


def split(re, im, axis):
    ar, br = halves(re, axis)
    ai, bi = halves(im, axis)
    re = jnp.concatenate([patched(ar + bi, ar, axis), patched(ar - bi, br, axis)], axis)
    im = jnp.concatenate([patched(ai - br, ai, axis), patched(ai + br, bi, axis)], axis)
    return re, im


def fold(re, im, axis):
    r1, r2 = halves(re, axis)
    i1, i2 = halves(im, axis)
    re = jnp.concatenate([patched(r1 + r2, r1, axis), patched(i2 - i1, r2, axis)], axis)
    im = jnp.concatenate([patched(i1 + i2, i1, axis), patched(r1 - r2, i2, axis)], axis)
    return re.astype(jnp.bfloat16), im.astype(jnp.bfloat16)


def mode_terms(ur, ui, probe_ref, mode, pr, pi, rows, cols):
    vr, vi = fold(dot(cols, ur), dot(cols, ui), 1)
    g = dot(jnp.concatenate([vr, vi], 0), rows)
    gr, gi = g[: g.shape[0] // 2], g[g.shape[0] // 2 :]
    qr = probe_ref[mode, 0].astype(jnp.float32)
    qi = probe_ref[mode, 1].astype(jnp.float32)
    return (
        (qr * gr + qi * gi, qr * gi - qi * gr),
        (pr * gr + pi * gi, pr * gi - pi * gr),
    )


def place_shares(meta_ref, probe_ref, pg_ref, keep_ref, send_ref, chunk, blocks):
    core, mode_bits, other_bits, base = (meta_ref[i] for i in (1, 3, 4, 5))
    modes, _, width, _ = probe_ref.shape
    share = modes // 2
    part = share // 2
    size = part * 2 * width // blocks
    starting = jnp.where(base == 1, 1.0, 0.0)

    def place(p, carry):
        here = pl.ds(pl.multiple_of(p * size, size), size)
        for target, at, bits, own in ((keep_ref, core, mode_bits, True), (send_ref, 1 - core, other_bits, False)):
            line = (p ^ bits) * size
            first = line // (2 * width)
            comp = line % (2 * width) // width
            inside = pl.ds(pl.multiple_of(line % width, size), size)
            value = -probe_rate * pg_ref[at * part + first, comp, inside]
            if own:
                value += starting * probe_ref[at * share + chunk * part + first, comp, inside].astype(jnp.float32)
            target[here] = value
        return carry

    lax.fori_loop(0, blocks, place, 0, unroll=blocks <= 8)


def chunk_modes(modes, chunk):
    part = modes // 4
    return [core * 2 * part + chunk * part + i for core in range(2) for i in range(part)]


def first_kernel(blocks, meta_ref, offs_ref, tile_ref, mine_ref, other_ref, probe_ref, amp_ref, table_ref,
                 keep_ref, send_ref, patch_ref, later_ref, acc_ref, pad_ref, far_ref, pg_ref):
    modes, _, width, _ = probe_ref.shape
    half = width // 2
    core, side = meta_ref[1], meta_ref[2]
    for source, at in ((mine_ref, core), (other_ref, 1 - core)):
        margin = pl.ds(pl.multiple_of(at * 3 * half, half), half)
        strip = pl.ds(pl.multiple_of((at + 1) * half, half), half)
        pad_ref[:, 1, margin] = source[:, :, :half]
        pad_ref[:, 2, margin] = source[:, :, half:width]
        for step in range(2):
            block = side if step == 0 else 3 - side
            start = width + step * width
            if start < source.shape[-1]:
                pad_ref[:, block, strip] = source[:, :, start : start + half]
                pad_ref[:, block, margin] = source[:, :, start + half : start + width]
            else:
                pad_ref[:, block, strip] = jnp.zeros((2, half, half), jnp.float32)
                pad_ref[:, block, margin] = jnp.zeros((2, half, half), jnp.float32)
    for j in range(2):
        pad_ref[:, 1 + j, half : half + width] = tile_ref[:, :, j * half : (j + 1) * half]
    pg_ref[...] = jnp.zeros_like(pg_ref)
    rows, cols = table_ref[0], table_ref[1]
    now, later = chunk_modes(modes, 0), chunk_modes(modes, 1)

    def visit(s, carry):
        row = offs_ref[0, s]
        col = offs_ref[1, s]
        block = jnp.where(col >= half, 1, 0)
        shift = col - block * half
        for comp in range(2):
            win = jnp.concatenate([pad_ref[comp, block + j, pl.ds(row, width), :] for j in range(3)], axis=1)
            patch_ref[s, comp] = pltpu.roll(win, lax.rem(width + half - shift, width + half), 1)[:, :width]
        inten = None
        for m in range(modes):
            qr = probe_ref[m, 0].astype(jnp.float32)
            qi = probe_ref[m, 1].astype(jnp.float32)
            pr = patch_ref[s, 0]
            pi = patch_ref[s, 1]
            psi_r = (qr * pr - qi * pi).astype(jnp.bfloat16)
            psi_i = (qr * pi + qi * pr).astype(jnp.bfloat16)
            yr, yi = split(dot(rows, psi_r), dot(rows, psi_i), 0)
            y = dot(jnp.concatenate([yr, yi], 0).astype(jnp.bfloat16), cols)
            fr, fi = split(y[:width], y[width:], 1)
            far_ref[m, 0] = fr
            far_ref[m, 1] = fi
            power = fr * fr + fi * fi
            inten = power if inten is None else inten + power
        scale = 1.0 / (width * width)
        factor = scale - amp_ref[s] * scale * lax.rsqrt(inten * scale + floor_term)
        total = None
        for m in now:
            ur, ui = fold(far_ref[m, 0] * factor, far_ref[m, 1] * factor, 0)
            at, term = mode_terms(ur, ui, probe_ref, m, patch_ref[s, 0], patch_ref[s, 1], rows, cols)
            total = at if total is None else (total[0] + at[0], total[1] + at[1])
            for comp in range(2):
                pg_ref[now.index(m), comp] += term[comp]
        for comp in range(2):
            acc_ref[s, comp] = total[comp]
        for m in later:
            ur, ui = fold(far_ref[m, 0] * factor, far_ref[m, 1] * factor, 0)
            later_ref[s, later.index(m), 0] = ur
            later_ref[s, later.index(m), 1] = ui
        return carry

    lax.fori_loop(0, meta_ref[0], visit, 0)
    place_shares(meta_ref, probe_ref, pg_ref, keep_ref, send_ref, 0, blocks)


def second_kernel(blocks, meta_ref, offs_ref, tile_ref, probe_ref, table_ref, patch_ref, later_ref, acc_ref,
                  keep_ref, send_ref, keep_grad_ref, send_grad_ref, grad_ref, pg_ref):
    modes, _, width, _ = probe_ref.shape
    half = width // 2
    core = meta_ref[1]
    grad_ref[...] = jnp.zeros_like(grad_ref)
    pg_ref[...] = jnp.zeros_like(pg_ref)
    rows, cols = table_ref[0], table_ref[1]
    later = chunk_modes(modes, 1)

    def visit(s, carry):
        row = offs_ref[0, s]
        col = offs_ref[1, s]
        block = jnp.where(col >= half, 1, 0)
        shift = col - block * half
        total = (acc_ref[s, 0], acc_ref[s, 1])
        for i, m in enumerate(later):
            at, term = mode_terms(later_ref[s, i, 0], later_ref[s, i, 1], probe_ref, m,
                                  patch_ref[s, 0], patch_ref[s, 1], rows, cols)
            total = (total[0] + at[0], total[1] + at[1])
            for comp in range(2):
                pg_ref[i, comp] += term[comp]
        for comp in range(2):
            wide = jnp.concatenate([total[comp], jnp.zeros((width, half), jnp.float32)], axis=1)
            wide = pltpu.roll(wide, shift, 1)
            for j in range(3):
                at = (comp, block + j, pl.ds(row, width), slice(None))
                grad_ref[at] = grad_ref[at] + wide[:, j * half : (j + 1) * half]
        return carry

    lax.fori_loop(0, meta_ref[0], visit, 0)
    place_shares(meta_ref, probe_ref, pg_ref, keep_ref, send_ref, 1, blocks)
    for target, at in ((keep_grad_ref, core), (send_grad_ref, 1 - core)):
        main = pl.ds(pl.multiple_of((at + 1) * half, half), half)
        margin = pl.ds(pl.multiple_of((1 - at) * 3 * half, half), half)
        target[0] = -field_rate * grad_ref[:, :, main]
        target[1] = -field_rate * grad_ref[:, :, margin]
    inner = pl.ds(pl.multiple_of(core * half, half), half)
    for j in range(2):
        keep_grad_ref[0, :, 1 + j] += tile_ref[:, inner, j * half : (j + 1) * half]


def prepare(probe, amp):
    width = probe.shape[-1]

    def body(probe_hbm, amp_hbm, probe_ref, amp_ref, table_ref, raw_ref, sems):
        copies = [
            pltpu.make_async_copy(source, target, sems.at[i])
            for i, (source, target) in enumerate([(amp_hbm, raw_ref), (probe_hbm, probe_ref)])
        ]
        for copy in copies:
            copy.start()
        for axis in range(2):
            table_ref[axis] = half_spectrum_table(width, axis)
        select = half_spectrum_select(width)
        copies[0].wait()

        def order(s, carry):
            amp_ref[s] = dot(dot(select, raw_ref[s]).astype(jnp.bfloat16), select)
            return carry

        lax.fori_loop(0, raw_ref.shape[0], order, 0)
        copies[1].wait()

    vmem = pl.BlockSpec(memory_space=pltpu.VMEM)
    hbm = pl.BlockSpec(memory_space=pl.ANY)
    return pl.pallas_call(
        body,
        out_shape=(
            jax.ShapeDtypeStruct(probe.shape, jnp.bfloat16),
            jax.ShapeDtypeStruct(amp.shape, jnp.float32),
            jax.ShapeDtypeStruct((2, width, width), jnp.bfloat16),
        ),
        in_specs=[hbm] * 2,
        out_specs=(vmem,) * 3,
        scratch_shapes=[
            pltpu.VMEM(amp.shape, jnp.bfloat16),
            pltpu.SemaphoreType.DMA((2,)),
        ],
        compiler_params=pltpu.CompilerParams(vmem_limit_bytes=51 * 2**20),
        cost_estimate=pl.CostEstimate(flops=2 * 10**8, bytes_accessed=4 * 2**20, transcendentals=0),
    )(probe, amp)


def first_scans(blocks, meta, offs, tile, mine, other, probe, amp, tables):
    modes, _, width, _ = probe.shape
    half = width // 2
    slots = amp.shape[0]
    part = modes // 4
    smem = pl.BlockSpec(memory_space=pltpu.SMEM)
    vmem = pl.BlockSpec(memory_space=pltpu.VMEM)
    share = jax.ShapeDtypeStruct((part * 2 * width, width), jnp.float32)
    image = jax.ShapeDtypeStruct((slots, 2, width, width), jnp.float32)
    return pl.pallas_call(
        functools.partial(first_kernel, blocks),
        out_shape=(share, share, image, jax.ShapeDtypeStruct((slots, 2 * part, 2, width, width), jnp.bfloat16), image),
        in_specs=[smem] * 2 + [vmem] * 6,
        out_specs=(vmem,) * 5,
        scratch_shapes=[
            pltpu.VMEM((2, 4, 2 * width, half), jnp.float32),
            pltpu.VMEM((modes, 2, width, width), jnp.float32),
            pltpu.VMEM((2 * part, 2, width, width), jnp.float32),
        ],
        compiler_params=pltpu.CompilerParams(vmem_limit_bytes=24 * 2**20),
        cost_estimate=pl.CostEstimate(flops=4 * 10**9, bytes_accessed=8 * 2**20, transcendentals=0),
    )(meta, offs, tile, mine, other, probe, amp, tables)


def second_scans(blocks, meta, offs, tile, probe, tables, patch, later, acc):
    modes, _, width, _ = probe.shape
    half = width // 2
    part = modes // 4
    smem = pl.BlockSpec(memory_space=pltpu.SMEM)
    vmem = pl.BlockSpec(memory_space=pltpu.VMEM)
    grad = jax.ShapeDtypeStruct((2, 2, 4, half, half), jnp.float32)
    share = jax.ShapeDtypeStruct((part * 2 * width, width), jnp.float32)
    return pl.pallas_call(
        functools.partial(second_kernel, blocks),
        out_shape=(share, share, grad, grad),
        in_specs=[smem] * 2 + [vmem] * 6,
        out_specs=(vmem,) * 4,
        scratch_shapes=[
            pltpu.VMEM((2, 4, 2 * width, half), jnp.float32),
            pltpu.VMEM((2 * part, 2, width, width), jnp.float32),
        ],
        compiler_params=pltpu.CompilerParams(vmem_limit_bytes=24 * 2**20),
        cost_estimate=pl.CostEstimate(flops=2 * 10**9, bytes_accessed=8 * 2**20, transcendentals=0),
    )(meta, offs, tile, probe, tables, patch, later, acc)


def route(target):
    rows, cols, cores = (lax.axis_size(a) for a in grid_axes)
    pairs = []
    for z in range(rows):
        for x in range(cols):
            for c in range(cores):
                to = target(z, x, c)
                if to is not None and 0 <= to[0] < rows and 0 <= to[1] < cols:
                    pairs.append(((z * cols + x) * cores + c, (to[0] * cols + to[1]) * cores + to[2]))
    return pairs


def move(block, target):
    return lax.ppermute(block, grid_axes, route(target))


def across(x, step):
    return x + 1 if x % 2 == step else x - 1


def down(z, c):
    return z + 1 if c == 0 else z - 1


def swap_cores(block):
    return move(block, lambda z, x, c: (z, x, 1 - c))


def axis_bits(axis):
    return [(axis, b) for b in range(lax.axis_size(axis).bit_length() - 1)]


def reduce_orders():
    first, second = axis_bits("yt"), axis_bits("xt")
    a, b = [], []
    for i in range(max(len(first), len(second))):
        pair = first[i : i + 1] + second[i : i + 1]
        a += pair
        b += pair[::-1]
    return list(zip(a, b))


def flip(order):
    def target(z, x, c):
        axis, bit = order[c]
        return (z ^ (1 << bit), x, c) if axis == "xt" else (z, x ^ (1 << bit), c)

    return target


def bits_of(orders, core):
    total = 0
    for order in orders:
        bits = [(lax.axis_index(axis) >> bit) & 1 for axis, bit in order]
        total = total * 2 + jnp.where(core == 0, bits[0], bits[1])
    return total


def small_call(body, outs, args):
    vmem = pl.BlockSpec(memory_space=pltpu.VMEM)
    return pl.pallas_call(
        body,
        out_shape=tuple(jax.ShapeDtypeStruct(shape, jnp.float32) for shape in outs),
        in_specs=[vmem] * len(args),
        out_specs=(vmem,) * len(outs),
        compiler_params=pltpu.CompilerParams(vmem_limit_bytes=6 * 2**20),
        cost_estimate=pl.CostEstimate(flops=10**6, bytes_accessed=2**20, transcendentals=0),
    )(*args)


def add_split(own, got):
    rows, lanes = own.shape
    cut = rows // 2

    def body(a, b, low, high):
        high[...] = a[cut:] + b[cut:]
        low[...] = a[:cut] + b[:cut]

    return small_call(body, [(cut, lanes)] * 2, [own, got])


def add(own, got):
    def body(a, b, out):
        out[...] = a[...] + b[...]

    return small_call(body, [own.shape], [own, got])[0]


def stack(own, got):
    rows, lanes = own.shape

    def body(a, b, out):
        out[:rows] = a[...]
        out[rows:] = b[...]

    return small_call(body, [(2 * rows, lanes)], [own, got])[0]


def strips(field, steps):
    _, tile, width = field.shape
    half = width // 2

    def body(tile_ref, outer_ref, *refs):
        sems = refs[-1]
        core, odd = lax.axis_index("sg"), lax.axis_index("yt") % 2
        outer = pl.ds(pl.multiple_of((1 - core) * half, half), half)
        inner = pl.ds(pl.multiple_of(core * half, half), half)
        copies = [pltpu.make_async_copy(tile_ref.at[:, outer], outer_ref, sems.at[0])]
        for step in range(steps):
            at = odd if step == 1 else 1 - odd
            cols = pl.ds(pl.multiple_of(at * half, half), half)
            for i, rows in enumerate((inner, outer)):
                n = 2 * step + i
                copies.append(pltpu.make_async_copy(tile_ref.at[:, rows, cols], refs[n], sems.at[1 + n]))
        for copy in copies:
            copy.start()
        for copy in copies:
            copy.wait()

    vmem = pl.BlockSpec(memory_space=pltpu.VMEM)
    shapes = [(2, half, width)] + [(2, half, half)] * (2 * steps)
    return pl.pallas_call(
        body,
        out_shape=tuple(jax.ShapeDtypeStruct(shape, jnp.float32) for shape in shapes),
        in_specs=[pl.BlockSpec(memory_space=pl.ANY)],
        out_specs=(vmem,) * len(shapes),
        scratch_shapes=[pltpu.SemaphoreType.DMA((1 + 2 * steps,))],
        compiler_params=pltpu.CompilerParams(vmem_limit_bytes=6 * 2**20),
        cost_estimate=pl.CostEstimate(flops=10**6, bytes_accessed=2**20, transcendentals=0),
    )(field)


def fold_sends(keep, got, steps):
    half = keep.shape[-1]

    def body(a, b, *refs):
        mid_ref, refs = refs[-1], refs[:-1]
        odd = lax.axis_index("yt") % 2
        for step in range(steps):
            block = 3 * (1 - odd) if step == 0 else 3 * odd
            refs[step][...] = a[:, :, block] + b[:, :, block]
        mid_ref[...] = a[:, :, 1:3] + b[:, :, 1:3]

    shapes = [(2, 2, half, half)] * steps + [(2, 2, 2, half, half)]
    *edges, mid = small_call(body, shapes, [keep, got])
    return edges, mid


def fold_join(mid, arrived):
    half = mid.shape[-1]

    def body(mid_ref, *refs):
        odd = lax.axis_index("yt") % 2
        down_ref, main_ref = refs[-2:]
        for j in range(2):
            total = mid_ref[:, :, j]
            for step, ref in enumerate(refs[:-2]):
                total += jnp.where((odd + step + j) % 2 == 1, 1.0, 0.0) * ref[...]
            main_ref[:, j] = total[0]
            down_ref[:, j] = total[1]

    return small_call(body, [(2, 2, half, half)] * 2, [mid, *arrived])


def fold_finish(main, below):
    half = main.shape[-1]

    def body(main_ref, below_ref, out_ref):
        for j in range(2):
            out_ref[:, :, j * half : (j + 1) * half] = main_ref[:, j] + below_ref[:, j]

    return small_call(body, [(2, half, 2 * half)], [main, below])[0]


def place_probe(chunks, early, blocks, shape, sibling, into=None):
    modes, _, width, _ = shape
    share = modes // 2
    part = share // 2
    size = part * 2 * width // blocks
    given = [] if into is None else [into]

    def body(*refs):
        sem = refs[-1]
        out_ref = refs[-2]
        core = lax.axis_index("sg")
        at = 1 - core if sibling else core
        bits = bits_of(early, at)

        def copies(p):
            found = []
            for k in range(2):
                line = ((at * share + k * part) * 2 * width) + (p ^ bits) * size
                target = out_ref.at[line // (2 * width), line % (2 * width) // width,
                                    pl.ds(pl.multiple_of(line % width, size), size)]
                here = refs[k].at[pl.ds(pl.multiple_of(p * size, size), size)]
                found.append(pltpu.make_async_copy(here, target, sem.at[p, k]))
            return found

        def start(p, carry):
            for copy in copies(p):
                copy.start()
            return carry

        def wait(p, carry):
            for copy in copies(p):
                copy.wait()
            return carry

        lax.fori_loop(0, blocks, start, 0)
        lax.fori_loop(0, blocks, wait, 0)

    anywhere = pl.BlockSpec(memory_space=pl.ANY)
    return pl.pallas_call(
        body,
        out_shape=jax.ShapeDtypeStruct(shape, jnp.float32),
        in_specs=[anywhere] * (2 + len(given)),
        out_specs=anywhere,
        input_output_aliases={2: 0} if given else {},
        scratch_shapes=[pltpu.SemaphoreType.DMA((blocks, 2))],
        compiler_params=pltpu.CompilerParams(vmem_limit_bytes=6 * 2**20),
        cost_estimate=pl.CostEstimate(flops=10**6, bytes_accessed=2**21, transcendentals=0),
    )(*chunks, *given)


def shards(field, probe, amplitudes, offsets, counts):
    modes, _, width, _ = probe.shape
    per_device = amplitudes.shape[2]
    core = lax.axis_index("sg")
    odd = lax.axis_index("yt") % 2
    steps = min(2, lax.axis_size("yt") - 1)
    orders = reduce_orders()
    early, last = orders[:-1], orders[-1]
    blocks = 2 ** len(early)
    live = jnp.clip(counts[0, 0] - core * per_device, 0, per_device)
    side = jnp.where(odd == 0, 3, 0)
    base = jnp.where((lax.axis_index("xt") == 0) & (lax.axis_index("yt") == 0), 1, 0)
    meta = jnp.stack(
        [live, core, side, bits_of(early, core), bits_of(early, 1 - core), base, odd]
    ).astype(jnp.int32)
    offs = offsets[0, 0].T

    outer, *edges = strips(field, steps)
    prepared = prepare(probe, amplitudes[0, 0])
    parts = [move(outer, lambda z, x, c: (down(z, c), x, c))]
    for step in range(steps):
        parts.append(move(edges[2 * step], lambda z, x, c: (z, across(x, step), c)))
        parts.append(move(edges[2 * step + 1], lambda z, x, c: (down(z, c), across(x, step), c)))
    parts, prepared, meta = lax.optimization_barrier((parts, prepared, meta))
    mine = jnp.concatenate(parts, axis=2)
    other = swap_cores(mine)

    probe_now, amp_now, tables = prepared
    keep, send, *kept = first_scans(blocks, meta, offs, field, mine, other, probe_now, amp_now, tables)
    second = second_scans(blocks, meta, offs, field, probe_now, tables, *kept)
    received, second = lax.optimization_barrier((swap_cores(send), second))
    keep2, send2, keep_grad, send_grad = second
    pairs = [add_split(keep, received), add_split(keep2, swap_cores(send2))]
    got = [move(high, flip(early[0])) for _, high in pairs]
    edges, mid = fold_sends(keep_grad, swap_cores(send_grad), steps)
    arrived = [
        move(edge, lambda z, x, c, step=step: (z, across(x, step), c)) for step, edge in enumerate(edges)
    ]
    for order in early[1:]:
        pairs = [add_split(low, g) for (low, _), g in zip(pairs, got)]
        got = [move(high, flip(order)) for _, high in pairs]
    parts = [add(low, g) for (low, _), g in zip(pairs, got)]
    parts = [add(p, move(p, flip(last))) for p in parts]
    parts[1], arrived = lax.optimization_barrier((parts[1], arrived))
    down_part, main = fold_join(mid, arrived)
    below = move(down_part, lambda z, x, c: (down(z, c), x, c))
    for order in early[::-1]:
        parts = [stack(p, move(p, flip(order))) for p in parts]
    parts[0], below = lax.optimization_barrier((parts[0], below))
    new_field = fold_finish(main, below)
    theirs = [swap_cores(p) for p in parts]
    new_probe = place_probe(parts, early, blocks, probe.shape, False)
    new_probe = place_probe(theirs, early, blocks, probe.shape, True, new_probe)
    return (new_field, new_probe)


def solution(mesh):
    in_specs = (
        P(None, ("groups", "xt"), "yt"),
        P("groups", None, None, None),
        P(("groups", "xt"), "yt", "sg", None, None),
        P(("groups", "xt"), "yt", "sg", None),
        P(("groups", "xt"), "yt"),
    )
    out_specs = (P(None, ("groups", "xt", "sg"), "yt"), P("groups", None, None, None))
    return jax.shard_map(shards, mesh=mesh, in_specs=in_specs, out_specs=out_specs, check_vma=False)
```

```python
import functools
import math

import jax
import jax.numpy as jnp
from jax import lax
from jax.experimental import pallas as pl
from jax.experimental.pallas import tpu as pltpu
from jax.sharding import PartitionSpec as P

floor_term = 0.5
field_rate = 0.25
probe_rate = 0.1
grid_axes = ("xt", "yt", "sg")


def cosine_of(phase, width):
    phase = phase & (width - 1)
    half = width // 2
    near = jnp.minimum(phase, width - phase)
    quarter = jnp.minimum(near, half - near)
    square = jnp.square(quarter.astype(jnp.float32) * (2.0 * math.pi / width))
    value = jnp.zeros_like(square)
    for power in range(12, -1, -2):
        value = value * square + (-1.0) ** (power // 2) / math.factorial(power)
    return jnp.where(near == quarter, value, -value)


def half_spectrum_table(width, axis):
    half = width // 2
    which = lax.broadcasted_iota(jnp.int32, (width, width), axis)
    other = lax.broadcasted_iota(jnp.int32, (width, width), 1 - axis)
    sine = which > half
    phase = jnp.where(sine, which - half, which) * other + jnp.where(sine, width - width // 4, 0)
    return cosine_of(phase, width).astype(jnp.bfloat16)


def half_spectrum_select(width):
    half = width // 2
    row = lax.broadcasted_iota(jnp.int32, (width, width), 0)
    col = lax.broadcasted_iota(jnp.int32, (width, width), 1)
    return (jnp.where(row > half, width + half - row, row) == col).astype(jnp.float32).astype(jnp.bfloat16)


def dot(a, b):
    return jnp.dot(a, b, preferred_element_type=jnp.float32)


def halves(x, axis):
    cut = x.shape[axis] // 2
    return (x[:cut], x[cut:]) if axis == 0 else (x[:, :cut], x[:, cut:])


def patched(general, special, axis):
    if axis == 0:
        first = lax.broadcasted_iota(jnp.int32, (8, general.shape[1]), 0) == 0
        return jnp.concatenate([jnp.where(first, special[:8], general[:8]), general[8:]], 0)
    first = lax.broadcasted_iota(jnp.int32, general.shape, 1) == 0
    return jnp.where(first, special, general)


def split(re, im, axis):
    ar, br = halves(re, axis)
    ai, bi = halves(im, axis)
    re = jnp.concatenate([patched(ar + bi, ar, axis), patched(ar - bi, br, axis)], axis)
    im = jnp.concatenate([patched(ai - br, ai, axis), patched(ai + br, bi, axis)], axis)
    return re, im


def fold(re, im, axis):
    r1, r2 = halves(re, axis)
    i1, i2 = halves(im, axis)
    re = jnp.concatenate([patched(r1 + r2, r1, axis), patched(i2 - i1, r2, axis)], axis)
    im = jnp.concatenate([patched(i1 + i2, i1, axis), patched(r1 - r2, i2, axis)], axis)
    return re.astype(jnp.bfloat16), im.astype(jnp.bfloat16)


def mode_terms(ur, ui, probe_ref, mode, pr, pi, rows, cols):
    vr, vi = fold(dot(cols, ur), dot(cols, ui), 1)
    gr, gi = dot(vr, rows), dot(vi, rows)
    qr = probe_ref[mode, 0].astype(jnp.float32)
    qi = probe_ref[mode, 1].astype(jnp.float32)
    return (
        (qr * gr + qi * gi, qr * gi - qi * gr),
        (pr * gr + pi * gi, pr * gi - pi * gr),
    )


def place_shares(meta_ref, probe_ref, pg_ref, keep_ref, send_ref, chunk, blocks):
    core, mode_bits, other_bits, base = (meta_ref[i] for i in (1, 3, 4, 5))
    modes, _, width, _ = probe_ref.shape
    share = modes // 2
    part = share // 2
    size = part * 2 * width // blocks
    starting = jnp.where(base == 1, 1.0, 0.0)

    def place(p, carry):
        here = pl.ds(pl.multiple_of(p * size, size), size)
        for target, at, bits, own in ((keep_ref, core, mode_bits, True), (send_ref, 1 - core, other_bits, False)):
            line = (p ^ bits) * size
            first = line // (2 * width)
            comp = line % (2 * width) // width
            inside = pl.ds(pl.multiple_of(line % width, size), size)
            value = -probe_rate * pg_ref[at * part + first, comp, inside]
            if own:
                value += starting * probe_ref[at * share + chunk * part + first, comp, inside].astype(jnp.float32)
            target[here] = value
        return carry

    lax.fori_loop(0, blocks, place, 0, unroll=blocks <= 8)


def chunk_modes(modes, chunk):
    part = modes // 4
    return [core * 2 * part + chunk * part + i for core in range(2) for i in range(part)]


def first_kernel(blocks, meta_ref, offs_ref, tile_ref, mine_ref, other_ref, probe_ref, amp_ref, table_ref,
                 keep_ref, send_ref, patch_ref, later_ref, acc_ref, pad_ref, far_ref, pg_ref):
    modes, _, width, _ = probe_ref.shape
    half = width // 2
    core, side = meta_ref[1], meta_ref[2]
    for source, at in ((mine_ref, core), (other_ref, 1 - core)):
        margin = pl.ds(pl.multiple_of(at * 3 * half, half), half)
        strip = pl.ds(pl.multiple_of((at + 1) * half, half), half)
        pad_ref[:, 1, margin] = source[:, :, :half]
        pad_ref[:, 2, margin] = source[:, :, half:width]
        for step in range(2):
            block = side if step == 0 else 3 - side
            start = width + step * width
            if start < source.shape[-1]:
                pad_ref[:, block, strip] = source[:, :, start : start + half]
                pad_ref[:, block, margin] = source[:, :, start + half : start + width]
            else:
                pad_ref[:, block, strip] = jnp.zeros((2, half, half), jnp.float32)
                pad_ref[:, block, margin] = jnp.zeros((2, half, half), jnp.float32)
    for j in range(2):
        pad_ref[:, 1 + j, half : half + width] = tile_ref[:, :, j * half : (j + 1) * half]
    pg_ref[...] = jnp.zeros_like(pg_ref)
    rows, cols = table_ref[0], table_ref[1]
    now, later = chunk_modes(modes, 0), chunk_modes(modes, 1)

    def visit(s, carry):
        row = offs_ref[0, s]
        col = offs_ref[1, s]
        block = jnp.where(col >= half, 1, 0)
        shift = col - block * half
        for comp in range(2):
            win = jnp.concatenate([pad_ref[comp, block + j, pl.ds(row, width), :] for j in range(3)], axis=1)
            patch_ref[s, comp] = pltpu.roll(win, lax.rem(width + half - shift, width + half), 1)[:, :width]
        inten = None
        for m in range(modes):
            qr = probe_ref[m, 0].astype(jnp.float32)
            qi = probe_ref[m, 1].astype(jnp.float32)
            pr = patch_ref[s, 0]
            pi = patch_ref[s, 1]
            psi_r = (qr * pr - qi * pi).astype(jnp.bfloat16)
            psi_i = (qr * pi + qi * pr).astype(jnp.bfloat16)
            yr, yi = split(dot(rows, psi_r), dot(rows, psi_i), 0)
            y = dot(jnp.concatenate([yr, yi], 0).astype(jnp.bfloat16), cols)
            fr, fi = split(y[:width], y[width:], 1)
            far_ref[m, 0] = fr
            far_ref[m, 1] = fi
            power = fr * fr + fi * fi
            inten = power if inten is None else inten + power
        scale = 1.0 / (width * width)
        factor = scale - amp_ref[s] * scale * lax.rsqrt(inten * scale + floor_term)
        total = None
        for m in now:
            ur, ui = fold(far_ref[m, 0] * factor, far_ref[m, 1] * factor, 0)
            at, term = mode_terms(ur, ui, probe_ref, m, patch_ref[s, 0], patch_ref[s, 1], rows, cols)
            total = at if total is None else (total[0] + at[0], total[1] + at[1])
            for comp in range(2):
                pg_ref[now.index(m), comp] += term[comp]
        for comp in range(2):
            acc_ref[s, comp] = total[comp]
        for m in later:
            ur, ui = fold(far_ref[m, 0] * factor, far_ref[m, 1] * factor, 0)
            later_ref[s, later.index(m), 0] = ur
            later_ref[s, later.index(m), 1] = ui
        return carry

    lax.fori_loop(0, meta_ref[0], visit, 0)
    place_shares(meta_ref, probe_ref, pg_ref, keep_ref, send_ref, 0, blocks)


def second_kernel(blocks, meta_ref, offs_ref, tile_ref, probe_ref, table_ref, patch_ref, later_ref, acc_ref,
                  keep_ref, send_ref, keep_grad_ref, send_grad_ref, grad_ref, pg_ref):
    modes, _, width, _ = probe_ref.shape
    half = width // 2
    core = meta_ref[1]
    grad_ref[...] = jnp.zeros_like(grad_ref)
    pg_ref[...] = jnp.zeros_like(pg_ref)
    rows, cols = table_ref[0], table_ref[1]
    later = chunk_modes(modes, 1)

    def visit(s, carry):
        row = offs_ref[0, s]
        col = offs_ref[1, s]
        block = jnp.where(col >= half, 1, 0)
        shift = col - block * half
        total = (acc_ref[s, 0], acc_ref[s, 1])
        for i, m in enumerate(later):
            at, term = mode_terms(later_ref[s, i, 0], later_ref[s, i, 1], probe_ref, m,
                                  patch_ref[s, 0], patch_ref[s, 1], rows, cols)
            total = (total[0] + at[0], total[1] + at[1])
            for comp in range(2):
                pg_ref[i, comp] += term[comp]
        for comp in range(2):
            wide = jnp.concatenate([total[comp], jnp.zeros((width, half), jnp.float32)], axis=1)
            wide = pltpu.roll(wide, shift, 1)
            for j in range(3):
                at = (comp, block + j, pl.ds(row, width), slice(None))
                grad_ref[at] = grad_ref[at] + wide[:, j * half : (j + 1) * half]
        return carry

    lax.fori_loop(0, meta_ref[0], visit, 0)
    place_shares(meta_ref, probe_ref, pg_ref, keep_ref, send_ref, 1, blocks)
    for target, at in ((keep_grad_ref, core), (send_grad_ref, 1 - core)):
        main = pl.ds(pl.multiple_of((at + 1) * half, half), half)
        margin = pl.ds(pl.multiple_of((1 - at) * 3 * half, half), half)
        target[0] = -field_rate * grad_ref[:, :, main]
        target[1] = -field_rate * grad_ref[:, :, margin]
    inner = pl.ds(pl.multiple_of(core * half, half), half)
    for j in range(2):
        keep_grad_ref[0, :, 1 + j] += tile_ref[:, inner, j * half : (j + 1) * half]


def prepare(probe, amp):
    width = probe.shape[-1]

    def body(probe_hbm, amp_hbm, probe_ref, amp_ref, table_ref, raw_ref, sems):
        copies = [
            pltpu.make_async_copy(source, target, sems.at[i])
            for i, (source, target) in enumerate([(amp_hbm, raw_ref), (probe_hbm, probe_ref)])
        ]
        for copy in copies:
            copy.start()
        for axis in range(2):
            table_ref[axis] = half_spectrum_table(width, axis)
        select = half_spectrum_select(width)
        copies[0].wait()

        def order(s, carry):
            amp_ref[s] = dot(dot(select, raw_ref[s]).astype(jnp.bfloat16), select)
            return carry

        lax.fori_loop(0, raw_ref.shape[0], order, 0)
        copies[1].wait()

    vmem = pl.BlockSpec(memory_space=pltpu.VMEM)
    hbm = pl.BlockSpec(memory_space=pl.ANY)
    return pl.pallas_call(
        body,
        out_shape=(
            jax.ShapeDtypeStruct(probe.shape, jnp.bfloat16),
            jax.ShapeDtypeStruct(amp.shape, jnp.float32),
            jax.ShapeDtypeStruct((2, width, width), jnp.bfloat16),
        ),
        in_specs=[hbm] * 2,
        out_specs=(vmem,) * 3,
        scratch_shapes=[
            pltpu.VMEM(amp.shape, jnp.bfloat16),
            pltpu.SemaphoreType.DMA((2,)),
        ],
        compiler_params=pltpu.CompilerParams(vmem_limit_bytes=51 * 2**20),
        cost_estimate=pl.CostEstimate(flops=2 * 10**8, bytes_accessed=4 * 2**20, transcendentals=0),
    )(probe, amp)


def first_scans(blocks, meta, offs, tile, mine, other, probe, amp, tables):
    modes, _, width, _ = probe.shape
    half = width // 2
    slots = amp.shape[0]
    part = modes // 4
    smem = pl.BlockSpec(memory_space=pltpu.SMEM)
    vmem = pl.BlockSpec(memory_space=pltpu.VMEM)
    share = jax.ShapeDtypeStruct((part * 2 * width, width), jnp.float32)
    image = jax.ShapeDtypeStruct((slots, 2, width, width), jnp.float32)
    return pl.pallas_call(
        functools.partial(first_kernel, blocks),
        out_shape=(share, share, image, jax.ShapeDtypeStruct((slots, 2 * part, 2, width, width), jnp.bfloat16), image),
        in_specs=[smem] * 2 + [vmem] * 6,
        out_specs=(vmem,) * 5,
        scratch_shapes=[
            pltpu.VMEM((2, 4, 2 * width, half), jnp.float32),
            pltpu.VMEM((modes, 2, width, width), jnp.float32),
            pltpu.VMEM((2 * part, 2, width, width), jnp.float32),
        ],
        compiler_params=pltpu.CompilerParams(vmem_limit_bytes=24 * 2**20),
        cost_estimate=pl.CostEstimate(flops=4 * 10**9, bytes_accessed=8 * 2**20, transcendentals=0),
    )(meta, offs, tile, mine, other, probe, amp, tables)


def second_scans(blocks, meta, offs, tile, probe, tables, patch, later, acc):
    modes, _, width, _ = probe.shape
    half = width // 2
    part = modes // 4
    smem = pl.BlockSpec(memory_space=pltpu.SMEM)
    vmem = pl.BlockSpec(memory_space=pltpu.VMEM)
    grad = jax.ShapeDtypeStruct((2, 2, 4, half, half), jnp.float32)
    share = jax.ShapeDtypeStruct((part * 2 * width, width), jnp.float32)
    return pl.pallas_call(
        functools.partial(second_kernel, blocks),
        out_shape=(share, share, grad, grad),
        in_specs=[smem] * 2 + [vmem] * 6,
        out_specs=(vmem,) * 4,
        scratch_shapes=[
            pltpu.VMEM((2, 4, 2 * width, half), jnp.float32),
            pltpu.VMEM((2 * part, 2, width, width), jnp.float32),
        ],
        compiler_params=pltpu.CompilerParams(vmem_limit_bytes=24 * 2**20),
        cost_estimate=pl.CostEstimate(flops=2 * 10**9, bytes_accessed=8 * 2**20, transcendentals=0),
    )(meta, offs, tile, probe, tables, patch, later, acc)


def route(target):
    rows, cols, cores = (lax.axis_size(a) for a in grid_axes)
    pairs = []
    for z in range(rows):
        for x in range(cols):
            for c in range(cores):
                to = target(z, x, c)
                if to is not None and 0 <= to[0] < rows and 0 <= to[1] < cols:
                    pairs.append(((z * cols + x) * cores + c, (to[0] * cols + to[1]) * cores + to[2]))
    return pairs


def move(block, target):
    return lax.ppermute(block, grid_axes, route(target))


def across(x, step):
    return x + 1 if x % 2 == step else x - 1


def down(z, c):
    return z + 1 if c == 0 else z - 1


def swap_cores(block):
    return move(block, lambda z, x, c: (z, x, 1 - c))


def axis_bits(axis):
    return [(axis, b) for b in range(lax.axis_size(axis).bit_length() - 1)]


def reduce_orders():
    first, second = axis_bits("yt"), axis_bits("xt")
    a, b = [], []
    for i in range(max(len(first), len(second))):
        pair = first[i : i + 1] + second[i : i + 1]
        a += pair
        b += pair[::-1]
    return list(zip(a, b))


def flip(order):
    def target(z, x, c):
        axis, bit = order[c]
        return (z ^ (1 << bit), x, c) if axis == "xt" else (z, x ^ (1 << bit), c)

    return target


def bits_of(orders, core):
    total = 0
    for order in orders:
        bits = [(lax.axis_index(axis) >> bit) & 1 for axis, bit in order]
        total = total * 2 + jnp.where(core == 0, bits[0], bits[1])
    return total


def small_call(body, outs, args):
    vmem = pl.BlockSpec(memory_space=pltpu.VMEM)
    return pl.pallas_call(
        body,
        out_shape=tuple(jax.ShapeDtypeStruct(shape, jnp.float32) for shape in outs),
        in_specs=[vmem] * len(args),
        out_specs=(vmem,) * len(outs),
        compiler_params=pltpu.CompilerParams(vmem_limit_bytes=6 * 2**20),
        cost_estimate=pl.CostEstimate(flops=10**6, bytes_accessed=2**20, transcendentals=0),
    )(*args)


def add_split(own, got):
    rows, lanes = own.shape
    cut = rows // 2

    def body(a, b, low, high):
        high[...] = a[cut:] + b[cut:]
        low[...] = a[:cut] + b[:cut]

    return small_call(body, [(cut, lanes)] * 2, [own, got])


def add(own, got):
    def body(a, b, out):
        out[...] = a[...] + b[...]

    return small_call(body, [own.shape], [own, got])[0]


def stack(own, got):
    rows, lanes = own.shape

    def body(a, b, out):
        out[:rows] = a[...]
        out[rows:] = b[...]

    return small_call(body, [(2 * rows, lanes)], [own, got])[0]


def strips(field, steps):
    _, tile, width = field.shape
    half = width // 2

    def body(tile_ref, outer_ref, *refs):
        sems = refs[-1]
        core, odd = lax.axis_index("sg"), lax.axis_index("yt") % 2
        outer = pl.ds(pl.multiple_of((1 - core) * half, half), half)
        inner = pl.ds(pl.multiple_of(core * half, half), half)
        copies = [pltpu.make_async_copy(tile_ref.at[:, outer], outer_ref, sems.at[0])]
        for step in range(steps):
            at = odd if step == 1 else 1 - odd
            cols = pl.ds(pl.multiple_of(at * half, half), half)
            for i, rows in enumerate((inner, outer)):
                n = 2 * step + i
                copies.append(pltpu.make_async_copy(tile_ref.at[:, rows, cols], refs[n], sems.at[1 + n]))
        for copy in copies:
            copy.start()
        for copy in copies:
            copy.wait()

    vmem = pl.BlockSpec(memory_space=pltpu.VMEM)
    shapes = [(2, half, width)] + [(2, half, half)] * (2 * steps)
    return pl.pallas_call(
        body,
        out_shape=tuple(jax.ShapeDtypeStruct(shape, jnp.float32) for shape in shapes),
        in_specs=[pl.BlockSpec(memory_space=pl.ANY)],
        out_specs=(vmem,) * len(shapes),
        scratch_shapes=[pltpu.SemaphoreType.DMA((1 + 2 * steps,))],
        compiler_params=pltpu.CompilerParams(vmem_limit_bytes=6 * 2**20),
        cost_estimate=pl.CostEstimate(flops=10**6, bytes_accessed=2**20, transcendentals=0),
    )(field)


def fold_sends(keep, got, steps):
    half = keep.shape[-1]

    def body(a, b, *refs):
        mid_ref, refs = refs[-1], refs[:-1]
        odd = lax.axis_index("yt") % 2
        for step in range(steps):
            block = 3 * (1 - odd) if step == 0 else 3 * odd
            refs[step][...] = a[:, :, block] + b[:, :, block]
        mid_ref[...] = a[:, :, 1:3] + b[:, :, 1:3]

    shapes = [(2, 2, half, half)] * steps + [(2, 2, 2, half, half)]
    *edges, mid = small_call(body, shapes, [keep, got])
    return edges, mid


def fold_join(mid, arrived):
    half = mid.shape[-1]

    def body(mid_ref, *refs):
        odd = lax.axis_index("yt") % 2
        down_ref, main_ref = refs[-2:]
        for j in range(2):
            total = mid_ref[:, :, j]
            for step, ref in enumerate(refs[:-2]):
                total += jnp.where((odd + step + j) % 2 == 1, 1.0, 0.0) * ref[...]
            main_ref[:, j] = total[0]
            down_ref[:, j] = total[1]

    return small_call(body, [(2, 2, half, half)] * 2, [mid, *arrived])


def fold_finish(main, below):
    half = main.shape[-1]

    def body(main_ref, below_ref, out_ref):
        for j in range(2):
            out_ref[:, :, j * half : (j + 1) * half] = main_ref[:, j] + below_ref[:, j]

    return small_call(body, [(2, half, 2 * half)], [main, below])[0]


def place_probe(chunks, early, blocks, shape, sibling, into=None):
    modes, _, width, _ = shape
    share = modes // 2
    part = share // 2
    size = part * 2 * width // blocks
    given = [] if into is None else [into]

    def body(*refs):
        sem = refs[-1]
        out_ref = refs[-2]
        core = lax.axis_index("sg")
        at = 1 - core if sibling else core
        bits = bits_of(early, at)

        def copies(p):
            found = []
            for k in range(2):
                line = ((at * share + k * part) * 2 * width) + (p ^ bits) * size
                target = out_ref.at[line // (2 * width), line % (2 * width) // width,
                                    pl.ds(pl.multiple_of(line % width, size), size)]
                here = refs[k].at[pl.ds(pl.multiple_of(p * size, size), size)]
                found.append(pltpu.make_async_copy(here, target, sem.at[p, k]))
            return found

        def start(p, carry):
            for copy in copies(p):
                copy.start()
            return carry

        def wait(p, carry):
            for copy in copies(p):
                copy.wait()
            return carry

        lax.fori_loop(0, blocks, start, 0)
        lax.fori_loop(0, blocks, wait, 0)

    anywhere = pl.BlockSpec(memory_space=pl.ANY)
    return pl.pallas_call(
        body,
        out_shape=jax.ShapeDtypeStruct(shape, jnp.float32),
        in_specs=[anywhere] * (2 + len(given)),
        out_specs=anywhere,
        input_output_aliases={2: 0} if given else {},
        scratch_shapes=[pltpu.SemaphoreType.DMA((blocks, 2))],
        compiler_params=pltpu.CompilerParams(vmem_limit_bytes=6 * 2**20),
        cost_estimate=pl.CostEstimate(flops=10**6, bytes_accessed=2**21, transcendentals=0),
    )(*chunks, *given)


def shards(field, probe, amplitudes, offsets, counts):
    modes, _, width, _ = probe.shape
    per_device = amplitudes.shape[2]
    core = lax.axis_index("sg")
    odd = lax.axis_index("yt") % 2
    steps = min(2, lax.axis_size("yt") - 1)
    orders = reduce_orders()
    early, last = orders[:-1], orders[-1]
    blocks = 2 ** len(early)
    live = jnp.clip(counts[0, 0] - core * per_device, 0, per_device)
    side = jnp.where(odd == 0, 3, 0)
    base = jnp.where((lax.axis_index("xt") == 0) & (lax.axis_index("yt") == 0), 1, 0)
    meta = jnp.stack(
        [live, core, side, bits_of(early, core), bits_of(early, 1 - core), base, odd]
    ).astype(jnp.int32)
    offs = offsets[0, 0].T

    outer, *edges = strips(field, steps)
    prepared = prepare(probe, amplitudes[0, 0])
    parts = [move(outer, lambda z, x, c: (down(z, c), x, c))]
    for step in range(steps):
        parts.append(move(edges[2 * step], lambda z, x, c: (z, across(x, step), c)))
        parts.append(move(edges[2 * step + 1], lambda z, x, c: (down(z, c), across(x, step), c)))
    parts, prepared, meta = lax.optimization_barrier((parts, prepared, meta))
    mine = jnp.concatenate(parts, axis=2)
    other = swap_cores(mine)

    probe_now, amp_now, tables = prepared
    keep, send, *kept = first_scans(blocks, meta, offs, field, mine, other, probe_now, amp_now, tables)
    second = second_scans(blocks, meta, offs, field, probe_now, tables, *kept)
    received, second = lax.optimization_barrier((swap_cores(send), second))
    keep2, send2, keep_grad, send_grad = second
    pairs = [add_split(keep, received), add_split(keep2, swap_cores(send2))]
    got = [move(high, flip(early[0])) for _, high in pairs]
    edges, mid = fold_sends(keep_grad, swap_cores(send_grad), steps)
    arrived = [
        move(edge, lambda z, x, c, step=step: (z, across(x, step), c)) for step, edge in enumerate(edges)
    ]
    for order in early[1:]:
        pairs = [add_split(low, g) for (low, _), g in zip(pairs, got)]
        got = [move(high, flip(order)) for _, high in pairs]
    parts = [add(low, g) for (low, _), g in zip(pairs, got)]
    parts = [add(p, move(p, flip(last))) for p in parts]
    parts[1], arrived = lax.optimization_barrier((parts[1], arrived))
    down_part, main = fold_join(mid, arrived)
    below = move(down_part, lambda z, x, c: (down(z, c), x, c))
    for order in early[::-1]:
        parts = [stack(p, move(p, flip(order))) for p in parts]
    parts[0], below = lax.optimization_barrier((parts[0], below))
    new_field = fold_finish(main, below)
    theirs = [swap_cores(p) for p in parts]
    new_probe = place_probe(parts, early, blocks, probe.shape, False)
    new_probe = place_probe(theirs, early, blocks, probe.shape, True, new_probe)
    return (new_field, new_probe)


def solution(mesh):
    in_specs = (
        P(None, ("groups", "xt"), "yt"),
        P("groups", None, None, None),
        P(("groups", "xt"), "yt", "sg", None, None),
        P(("groups", "xt"), "yt", "sg", None),
        P(("groups", "xt"), "yt"),
    )
    out_specs = (P(None, ("groups", "xt", "sg"), "yt"), P("groups", None, None, None))
    return jax.shard_map(shards, mesh=mesh, in_specs=in_specs, out_specs=out_specs, check_vma=False)
```

```python
import functools
import math

import jax
import jax.numpy as jnp
from jax import lax
from jax.experimental import pallas as pl
from jax.experimental.pallas import tpu as pltpu
from jax.sharding import PartitionSpec as P

floor_term = 0.5
field_rate = 0.25
probe_rate = 0.1
grid_axes = ("xt", "yt", "sg")


def cosine_of(phase, width):
    phase = phase & (width - 1)
    half = width // 2
    near = jnp.minimum(phase, width - phase)
    quarter = jnp.minimum(near, half - near)
    square = jnp.square(quarter.astype(jnp.float32) * (2.0 * math.pi / width))
    value = jnp.zeros_like(square)
    for power in range(12, -1, -2):
        value = value * square + (-1.0) ** (power // 2) / math.factorial(power)
    return jnp.where(near == quarter, value, -value)


def half_spectrum_table(width, axis):
    half = width // 2
    which = lax.broadcasted_iota(jnp.int32, (width, width), axis)
    other = lax.broadcasted_iota(jnp.int32, (width, width), 1 - axis)
    sine = which > half
    phase = jnp.where(sine, which - half, which) * other + jnp.where(sine, width - width // 4, 0)
    return cosine_of(phase, width).astype(jnp.bfloat16)


def half_spectrum_select(width):
    half = width // 2
    row = lax.broadcasted_iota(jnp.int32, (width, width), 0)
    col = lax.broadcasted_iota(jnp.int32, (width, width), 1)
    return (jnp.where(row > half, width + half - row, row) == col).astype(jnp.float32).astype(jnp.bfloat16)


def dot(a, b):
    return jnp.dot(a, b, preferred_element_type=jnp.float32)


def halves(x, axis):
    cut = x.shape[axis] // 2
    return (x[:cut], x[cut:]) if axis == 0 else (x[:, :cut], x[:, cut:])


def patched(general, special, axis):
    if axis == 0:
        first = lax.broadcasted_iota(jnp.int32, (8, general.shape[1]), 0) == 0
        return jnp.concatenate([jnp.where(first, special[:8], general[:8]), general[8:]], 0)
    first = lax.broadcasted_iota(jnp.int32, general.shape, 1) == 0
    return jnp.where(first, special, general)


def split(re, im, axis):
    ar, br = halves(re, axis)
    ai, bi = halves(im, axis)
    re = jnp.concatenate([patched(ar + bi, ar, axis), patched(ar - bi, br, axis)], axis)
    im = jnp.concatenate([patched(ai - br, ai, axis), patched(ai + br, bi, axis)], axis)
    return re, im


def fold(re, im, axis):
    r1, r2 = halves(re, axis)
    i1, i2 = halves(im, axis)
    re = jnp.concatenate([patched(r1 + r2, r1, axis), patched(i2 - i1, r2, axis)], axis)
    im = jnp.concatenate([patched(i1 + i2, i1, axis), patched(r1 - r2, i2, axis)], axis)
    return re.astype(jnp.bfloat16), im.astype(jnp.bfloat16)


def mode_terms(ur, ui, probe_ref, mode, pr, pi, rows, cols):
    vr, vi = fold(dot(cols, ur), dot(cols, ui), 1)
    gr, gi = dot(vr, rows), dot(vi, rows)
    qr = probe_ref[mode, 0].astype(jnp.float32)
    qi = probe_ref[mode, 1].astype(jnp.float32)
    return (
        (qr * gr + qi * gi, qr * gi - qi * gr),
        (pr * gr + pi * gi, pr * gi - pi * gr),
    )


def place_shares(meta_ref, probe_ref, pg_ref, keep_ref, send_ref, chunk, blocks):
    core, mode_bits, other_bits, base = (meta_ref[i] for i in (1, 3, 4, 5))
    modes, _, width, _ = probe_ref.shape
    share = modes // 2
    part = share // 2
    size = part * 2 * width // blocks
    starting = jnp.where(base == 1, 1.0, 0.0)

    def place(p, carry):
        here = pl.ds(pl.multiple_of(p * size, size), size)
        for target, at, bits, own in ((keep_ref, core, mode_bits, True), (send_ref, 1 - core, other_bits, False)):
            line = (p ^ bits) * size
            first = line // (2 * width)
            comp = line % (2 * width) // width
            inside = pl.ds(pl.multiple_of(line % width, size), size)
            value = -probe_rate * pg_ref[at * part + first, comp, inside]
            if own:
                value += starting * probe_ref[at * share + chunk * part + first, comp, inside].astype(jnp.float32)
            target[here] = value
        return carry

    lax.fori_loop(0, blocks, place, 0, unroll=blocks <= 8)


def chunk_modes(modes, chunk):
    part = modes // 4
    return [core * 2 * part + chunk * part + i for core in range(2) for i in range(part)]


def first_kernel(blocks, meta_ref, offs_ref, tile_ref, mine_ref, other_ref, probe_ref, amp_ref, table_ref,
                 keep_ref, send_ref, patch_ref, later_ref, acc_ref, pad_ref, far_ref, pg_ref):
    modes, _, width, _ = probe_ref.shape
    half = width // 2
    core, side = meta_ref[1], meta_ref[2]
    for source, at in ((mine_ref, core), (other_ref, 1 - core)):
        margin = pl.ds(pl.multiple_of(at * 3 * half, half), half)
        strip = pl.ds(pl.multiple_of((at + 1) * half, half), half)
        pad_ref[:, 1, margin] = source[:, :, :half]
        pad_ref[:, 2, margin] = source[:, :, half:width]
        for step in range(2):
            block = side if step == 0 else 3 - side
            start = width + step * width
            if start < source.shape[-1]:
                pad_ref[:, block, strip] = source[:, :, start : start + half]
                pad_ref[:, block, margin] = source[:, :, start + half : start + width]
            else:
                pad_ref[:, block, strip] = jnp.zeros((2, half, half), jnp.float32)
                pad_ref[:, block, margin] = jnp.zeros((2, half, half), jnp.float32)
    for j in range(2):
        pad_ref[:, 1 + j, half : half + width] = tile_ref[:, :, j * half : (j + 1) * half]
    pg_ref[...] = jnp.zeros_like(pg_ref)
    rows, cols = table_ref[0], table_ref[1]
    now, later = chunk_modes(modes, 0), chunk_modes(modes, 1)

    def visit(s, carry):
        row = offs_ref[0, s]
        col = offs_ref[1, s]
        block = jnp.where(col >= half, 1, 0)
        shift = col - block * half
        for comp in range(2):
            win = jnp.concatenate([pad_ref[comp, block + j, pl.ds(row, width), :] for j in range(3)], axis=1)
            patch_ref[s, comp] = pltpu.roll(win, lax.rem(width + half - shift, width + half), 1)[:, :width]
        inten = None
        for m in range(modes):
            qr = probe_ref[m, 0].astype(jnp.float32)
            qi = probe_ref[m, 1].astype(jnp.float32)
            pr = patch_ref[s, 0]
            pi = patch_ref[s, 1]
            psi_r = (qr * pr - qi * pi).astype(jnp.bfloat16)
            psi_i = (qr * pi + qi * pr).astype(jnp.bfloat16)
            yr, yi = split(dot(rows, psi_r), dot(rows, psi_i), 0)
            y = dot(jnp.concatenate([yr, yi], 0).astype(jnp.bfloat16), cols)
            fr, fi = split(y[:width], y[width:], 1)
            far_ref[m, 0] = fr
            far_ref[m, 1] = fi
            power = fr * fr + fi * fi
            inten = power if inten is None else inten + power
        scale = 1.0 / (width * width)
        factor = scale - amp_ref[s] * scale * lax.rsqrt(inten * scale + floor_term)
        total = None
        for m in now:
            ur, ui = fold(far_ref[m, 0] * factor, far_ref[m, 1] * factor, 0)
            at, term = mode_terms(ur, ui, probe_ref, m, patch_ref[s, 0], patch_ref[s, 1], rows, cols)
            total = at if total is None else (total[0] + at[0], total[1] + at[1])
            for comp in range(2):
                pg_ref[now.index(m), comp] += term[comp]
        for comp in range(2):
            acc_ref[s, comp] = total[comp]
        for m in later:
            ur, ui = fold(far_ref[m, 0] * factor, far_ref[m, 1] * factor, 0)
            later_ref[s, later.index(m), 0] = ur
            later_ref[s, later.index(m), 1] = ui
        return carry

    lax.fori_loop(0, meta_ref[0], visit, 0)
    place_shares(meta_ref, probe_ref, pg_ref, keep_ref, send_ref, 0, blocks)


def second_kernel(blocks, meta_ref, offs_ref, tile_ref, probe_ref, table_ref, patch_ref, later_ref, acc_ref,
                  keep_ref, send_ref, keep_grad_ref, send_grad_ref, grad_ref, pg_ref):
    modes, _, width, _ = probe_ref.shape
    half = width // 2
    core = meta_ref[1]
    grad_ref[...] = jnp.zeros_like(grad_ref)
    pg_ref[...] = jnp.zeros_like(pg_ref)
    rows, cols = table_ref[0], table_ref[1]
    later = chunk_modes(modes, 1)

    def visit(s, carry):
        row = offs_ref[0, s]
        col = offs_ref[1, s]
        block = jnp.where(col >= half, 1, 0)
        shift = col - block * half
        total = (acc_ref[s, 0], acc_ref[s, 1])
        for i, m in enumerate(later):
            at, term = mode_terms(later_ref[s, i, 0], later_ref[s, i, 1], probe_ref, m,
                                  patch_ref[s, 0], patch_ref[s, 1], rows, cols)
            total = (total[0] + at[0], total[1] + at[1])
            for comp in range(2):
                pg_ref[i, comp] += term[comp]
        for comp in range(2):
            wide = jnp.concatenate([total[comp], jnp.zeros((width, half), jnp.float32)], axis=1)
            wide = pltpu.roll(wide, shift, 1)
            for j in range(3):
                at = (comp, block + j, pl.ds(row, width), slice(None))
                grad_ref[at] = grad_ref[at] + wide[:, j * half : (j + 1) * half]
        return carry

    lax.fori_loop(0, meta_ref[0], visit, 0)
    place_shares(meta_ref, probe_ref, pg_ref, keep_ref, send_ref, 1, blocks)
    for target, at in ((keep_grad_ref, core), (send_grad_ref, 1 - core)):
        main = pl.ds(pl.multiple_of((at + 1) * half, half), half)
        margin = pl.ds(pl.multiple_of((1 - at) * 3 * half, half), half)
        target[0] = -field_rate * grad_ref[:, :, main]
        target[1] = -field_rate * grad_ref[:, :, margin]
    inner = pl.ds(pl.multiple_of(core * half, half), half)
    for j in range(2):
        keep_grad_ref[0, :, 1 + j] += tile_ref[:, inner, j * half : (j + 1) * half]


def prepare(probe, amp):
    width = probe.shape[-1]

    def body(probe_hbm, amp_hbm, probe_ref, amp_ref, table_ref, raw_ref, sems):
        copies = [
            pltpu.make_async_copy(source, target, sems.at[i])
            for i, (source, target) in enumerate([(amp_hbm, raw_ref), (probe_hbm, probe_ref)])
        ]
        for copy in copies:
            copy.start()
        for axis in range(2):
            table_ref[axis] = half_spectrum_table(width, axis)
        select = half_spectrum_select(width)
        copies[0].wait()

        def order(s, carry):
            amp_ref[s] = dot(dot(select, raw_ref[s]).astype(jnp.bfloat16), select)
            return carry

        lax.fori_loop(0, raw_ref.shape[0], order, 0)
        copies[1].wait()

    vmem = pl.BlockSpec(memory_space=pltpu.VMEM)
    hbm = pl.BlockSpec(memory_space=pl.ANY)
    return pl.pallas_call(
        body,
        out_shape=(
            jax.ShapeDtypeStruct(probe.shape, jnp.bfloat16),
            jax.ShapeDtypeStruct(amp.shape, jnp.float32),
            jax.ShapeDtypeStruct((2, width, width), jnp.bfloat16),
        ),
        in_specs=[hbm] * 2,
        out_specs=(vmem,) * 3,
        scratch_shapes=[
            pltpu.VMEM(amp.shape, jnp.bfloat16),
            pltpu.SemaphoreType.DMA((2,)),
        ],
        compiler_params=pltpu.CompilerParams(vmem_limit_bytes=51 * 2**20),
        cost_estimate=pl.CostEstimate(flops=2 * 10**8, bytes_accessed=4 * 2**20, transcendentals=0),
    )(probe, amp)


def first_scans(blocks, meta, offs, tile, mine, other, probe, amp, tables):
    modes, _, width, _ = probe.shape
    half = width // 2
    slots = amp.shape[0]
    part = modes // 4
    smem = pl.BlockSpec(memory_space=pltpu.SMEM)
    vmem = pl.BlockSpec(memory_space=pltpu.VMEM)
    share = jax.ShapeDtypeStruct((part * 2 * width, width), jnp.float32)
    image = jax.ShapeDtypeStruct((slots, 2, width, width), jnp.float32)
    return pl.pallas_call(
        functools.partial(first_kernel, blocks),
        out_shape=(share, share, image, jax.ShapeDtypeStruct((slots, 2 * part, 2, width, width), jnp.bfloat16), image),
        in_specs=[smem] * 2 + [vmem] * 6,
        out_specs=(vmem,) * 5,
        scratch_shapes=[
            pltpu.VMEM((2, 4, 2 * width, half), jnp.float32),
            pltpu.VMEM((modes, 2, width, width), jnp.float32),
            pltpu.VMEM((2 * part, 2, width, width), jnp.float32),
        ],
        compiler_params=pltpu.CompilerParams(vmem_limit_bytes=24 * 2**20),
        cost_estimate=pl.CostEstimate(flops=4 * 10**9, bytes_accessed=8 * 2**20, transcendentals=0),
    )(meta, offs, tile, mine, other, probe, amp, tables)


def second_scans(blocks, meta, offs, tile, probe, tables, patch, later, acc):
    modes, _, width, _ = probe.shape
    half = width // 2
    part = modes // 4
    smem = pl.BlockSpec(memory_space=pltpu.SMEM)
    vmem = pl.BlockSpec(memory_space=pltpu.VMEM)
    grad = jax.ShapeDtypeStruct((2, 2, 4, half, half), jnp.float32)
    share = jax.ShapeDtypeStruct((part * 2 * width, width), jnp.float32)
    return pl.pallas_call(
        functools.partial(second_kernel, blocks),
        out_shape=(share, share, grad, grad),
        in_specs=[smem] * 2 + [vmem] * 6,
        out_specs=(vmem,) * 4,
        scratch_shapes=[
            pltpu.VMEM((2, 4, 2 * width, half), jnp.float32),
            pltpu.VMEM((2 * part, 2, width, width), jnp.float32),
        ],
        compiler_params=pltpu.CompilerParams(vmem_limit_bytes=24 * 2**20),
        cost_estimate=pl.CostEstimate(flops=2 * 10**9, bytes_accessed=8 * 2**20, transcendentals=0),
    )(meta, offs, tile, probe, tables, patch, later, acc)


def route(target):
    rows, cols, cores = (lax.axis_size(a) for a in grid_axes)
    pairs = []
    for z in range(rows):
        for x in range(cols):
            for c in range(cores):
                to = target(z, x, c)
                if to is not None and 0 <= to[0] < rows and 0 <= to[1] < cols:
                    pairs.append(((z * cols + x) * cores + c, (to[0] * cols + to[1]) * cores + to[2]))
    return pairs


def move(block, target):
    return lax.ppermute(block, grid_axes, route(target))


def across(x, step):
    return x + 1 if x % 2 == step else x - 1


def down(z, c):
    return z + 1 if c == 0 else z - 1


def swap_cores(block):
    return move(block, lambda z, x, c: (z, x, 1 - c))


def axis_bits(axis):
    return [(axis, b) for b in range(lax.axis_size(axis).bit_length() - 1)]


def reduce_orders():
    first, second = axis_bits("yt"), axis_bits("xt")
    a, b = [], []
    for i in range(max(len(first), len(second))):
        pair = first[i : i + 1] + second[i : i + 1]
        a += pair
        b += pair[::-1]
    return list(zip(a, b))


def flip(order):
    def target(z, x, c):
        axis, bit = order[c]
        return (z ^ (1 << bit), x, c) if axis == "xt" else (z, x ^ (1 << bit), c)

    return target


def bits_of(orders, core):
    total = 0
    for order in orders:
        bits = [(lax.axis_index(axis) >> bit) & 1 for axis, bit in order]
        total = total * 2 + jnp.where(core == 0, bits[0], bits[1])
    return total


def small_call(body, outs, args):
    vmem = pl.BlockSpec(memory_space=pltpu.VMEM)
    return pl.pallas_call(
        body,
        out_shape=tuple(jax.ShapeDtypeStruct(shape, jnp.float32) for shape in outs),
        in_specs=[vmem] * len(args),
        out_specs=(vmem,) * len(outs),
        compiler_params=pltpu.CompilerParams(vmem_limit_bytes=6 * 2**20),
        cost_estimate=pl.CostEstimate(flops=10**6, bytes_accessed=2**20, transcendentals=0),
    )(*args)


def add_split(own, got):
    rows, lanes = own.shape
    cut = rows // 2

    def body(a, b, low, high):
        high[...] = a[cut:] + b[cut:]
        low[...] = a[:cut] + b[:cut]

    return small_call(body, [(cut, lanes)] * 2, [own, got])


def add(own, got):
    def body(a, b, out):
        out[...] = a[...] + b[...]

    return small_call(body, [own.shape], [own, got])[0]


def stack(own, got):
    rows, lanes = own.shape

    def body(a, b, out):
        out[:rows] = a[...]
        out[rows:] = b[...]

    return small_call(body, [(2 * rows, lanes)], [own, got])[0]


def strips(field, steps):
    _, tile, width = field.shape
    half = width // 2

    def body(tile_ref, outer_ref, *refs):
        sems = refs[-1]
        core, odd = lax.axis_index("sg"), lax.axis_index("yt") % 2
        outer = pl.ds(pl.multiple_of((1 - core) * half, half), half)
        inner = pl.ds(pl.multiple_of(core * half, half), half)
        copies = [pltpu.make_async_copy(tile_ref.at[:, outer], outer_ref, sems.at[0])]
        for step in range(steps):
            at = odd if step == 1 else 1 - odd
            cols = pl.ds(pl.multiple_of(at * half, half), half)
            for i, rows in enumerate((inner, outer)):
                n = 2 * step + i
                copies.append(pltpu.make_async_copy(tile_ref.at[:, rows, cols], refs[n], sems.at[1 + n]))
        for copy in copies:
            copy.start()
        for copy in copies:
            copy.wait()

    vmem = pl.BlockSpec(memory_space=pltpu.VMEM)
    shapes = [(2, half, width)] + [(2, half, half)] * (2 * steps)
    return pl.pallas_call(
        body,
        out_shape=tuple(jax.ShapeDtypeStruct(shape, jnp.float32) for shape in shapes),
        in_specs=[pl.BlockSpec(memory_space=pl.ANY)],
        out_specs=(vmem,) * len(shapes),
        scratch_shapes=[pltpu.SemaphoreType.DMA((1 + 2 * steps,))],
        compiler_params=pltpu.CompilerParams(vmem_limit_bytes=6 * 2**20),
        cost_estimate=pl.CostEstimate(flops=10**6, bytes_accessed=2**20, transcendentals=0),
    )(field)


def fold_sends(keep, got, steps):
    half = keep.shape[-1]

    def body(a, b, *refs):
        mid_ref, refs = refs[-1], refs[:-1]
        odd = lax.axis_index("yt") % 2
        for step in range(steps):
            block = 3 * (1 - odd) if step == 0 else 3 * odd
            refs[step][...] = a[:, :, block] + b[:, :, block]
        mid_ref[...] = a[:, :, 1:3] + b[:, :, 1:3]

    shapes = [(2, 2, half, half)] * steps + [(2, 2, 2, half, half)]
    *edges, mid = small_call(body, shapes, [keep, got])
    return edges, mid


def fold_join(mid, arrived):
    half = mid.shape[-1]

    def body(mid_ref, *refs):
        odd = lax.axis_index("yt") % 2
        down_ref, main_ref = refs[-2:]
        for j in range(2):
            total = mid_ref[:, :, j]
            for step, ref in enumerate(refs[:-2]):
                total += jnp.where((odd + step + j) % 2 == 1, 1.0, 0.0) * ref[...]
            main_ref[:, j] = total[0]
            down_ref[:, j] = total[1]

    return small_call(body, [(2, 2, half, half)] * 2, [mid, *arrived])


def fold_finish(main, below):
    half = main.shape[-1]

    def body(main_ref, below_ref, out_ref):
        for j in range(2):
            out_ref[:, :, j * half : (j + 1) * half] = main_ref[:, j] + below_ref[:, j]

    return small_call(body, [(2, half, 2 * half)], [main, below])[0]


def place_probe(chunks, early, blocks, shape, sibling, into=None):
    modes, _, width, _ = shape
    share = modes // 2
    part = share // 2
    size = part * 2 * width // blocks
    given = [] if into is None else [into]

    def body(*refs):
        sem = refs[-1]
        out_ref = refs[-2]
        core = lax.axis_index("sg")
        at = 1 - core if sibling else core
        bits = bits_of(early, at)

        def copies(p):
            found = []
            for k in range(2):
                line = ((at * share + k * part) * 2 * width) + (p ^ bits) * size
                target = out_ref.at[line // (2 * width), line % (2 * width) // width,
                                    pl.ds(pl.multiple_of(line % width, size), size)]
                here = refs[k].at[pl.ds(pl.multiple_of(p * size, size), size)]
                found.append(pltpu.make_async_copy(here, target, sem.at[p, k]))
            return found

        def start(p, carry):
            for copy in copies(p):
                copy.start()
            return carry

        def wait(p, carry):
            for copy in copies(p):
                copy.wait()
            return carry

        lax.fori_loop(0, blocks, start, 0)
        lax.fori_loop(0, blocks, wait, 0)

    anywhere = pl.BlockSpec(memory_space=pl.ANY)
    return pl.pallas_call(
        body,
        out_shape=jax.ShapeDtypeStruct(shape, jnp.float32),
        in_specs=[anywhere] * (2 + len(given)),
        out_specs=anywhere,
        input_output_aliases={2: 0} if given else {},
        scratch_shapes=[pltpu.SemaphoreType.DMA((blocks, 2))],
        compiler_params=pltpu.CompilerParams(vmem_limit_bytes=6 * 2**20),
        cost_estimate=pl.CostEstimate(flops=10**6, bytes_accessed=2**21, transcendentals=0),
    )(*chunks, *given)


def shards(field, probe, amplitudes, offsets, counts):
    modes, _, width, _ = probe.shape
    per_device = amplitudes.shape[2]
    core = lax.axis_index("sg")
    odd = lax.axis_index("yt") % 2
    steps = min(2, lax.axis_size("yt") - 1)
    orders = reduce_orders()
    early, last = orders[:-1], orders[-1]
    blocks = 2 ** len(early)
    live = jnp.clip(counts[0, 0] - core * per_device, 0, per_device)
    side = jnp.where(odd == 0, 3, 0)
    base = jnp.where((lax.axis_index("xt") == 0) & (lax.axis_index("yt") == 0), 1, 0)
    meta = jnp.stack(
        [live, core, side, bits_of(early, core), bits_of(early, 1 - core), base, odd]
    ).astype(jnp.int32)
    offs = offsets[0, 0].T

    outer, *edges = strips(field, steps)
    prepared = prepare(probe, amplitudes[0, 0])
    parts = [move(outer, lambda z, x, c: (down(z, c), x, c))]
    for step in range(steps):
        parts.append(move(edges[2 * step], lambda z, x, c: (z, across(x, step), c)))
        parts.append(move(edges[2 * step + 1], lambda z, x, c: (down(z, c), across(x, step), c)))
    parts, prepared, meta = lax.optimization_barrier((parts, prepared, meta))
    mine = jnp.concatenate(parts, axis=2)
    other = swap_cores(mine)

    probe_now, amp_now, tables = prepared
    keep, send, *kept = first_scans(blocks, meta, offs, field, mine, other, probe_now, amp_now, tables)
    second = second_scans(blocks, meta, offs, field, probe_now, tables, *kept)
    received, second = lax.optimization_barrier((swap_cores(send), second))
    keep2, send2, keep_grad, send_grad = second
    pairs = [add_split(keep, received), add_split(keep2, swap_cores(send2))]
    got = [move(high, flip(early[0])) for _, high in pairs]
    edges, mid = fold_sends(keep_grad, swap_cores(send_grad), steps)
    arrived = [
        move(edge, lambda z, x, c, step=step: (z, across(x, step), c)) for step, edge in enumerate(edges)
    ]
    for order in early[1:]:
        pairs = [add_split(low, g) for (low, _), g in zip(pairs, got)]
        got = [move(high, flip(order)) for _, high in pairs]
    parts = [add(low, g) for (low, _), g in zip(pairs, got)]
    parts = [add(p, move(p, flip(last))) for p in parts]
    parts[1], arrived = lax.optimization_barrier((parts[1], arrived))
    down_part, main = fold_join(mid, arrived)
    below = move(down_part, lambda z, x, c: (down(z, c), x, c))
    for order in early[::-1]:
        parts = [stack(p, move(p, flip(order))) for p in parts]
    parts[1], below = lax.optimization_barrier((parts[1], below))
    new_field = fold_finish(main, below)
    theirs = [swap_cores(p) for p in parts]
    new_probe = place_probe(parts, early, blocks, probe.shape, False)
    new_probe = place_probe(theirs, early, blocks, probe.shape, True, new_probe)
    return (new_field, new_probe)


def solution(mesh):
    in_specs = (
        P(None, ("groups", "xt"), "yt"),
        P("groups", None, None, None),
        P(("groups", "xt"), "yt", "sg", None, None),
        P(("groups", "xt"), "yt", "sg", None),
        P(("groups", "xt"), "yt"),
    )
    out_specs = (P(None, ("groups", "xt", "sg"), "yt"), P("groups", None, None, None))
    return jax.shard_map(shards, mesh=mesh, in_specs=in_specs, out_specs=out_specs, check_vma=False)
```
